32 devices in a mesh: shell: 16 (over z, y, x), sky: 2 (over core).
Axes of the slice: x: 2, y: 2, z: 4, core: 2. Of those that a mesh axis runs over, the one named last changes fastest.
Arguments:
- excitation: float32 [512, 65536], P('shell', 'sky'), may hold values from -1.8 to 1.8
- star_shell: int32 [32, 32, 128], P(('shell', 'sky')), may hold values from 0 to 31
- star_pixel: int32 [32, 32, 128], P(('shell', 'sky')), may hold values from 0 to 32767
- star_fraction: float32 [32, 32, 128], P(('shell', 'sky')), may hold values from 0 to 1
- star_count: int32 [32, 32], P(('shell', 'sky')), may hold values from 0 to 128, as said below
- observed: float32 [32, 32, 128], P(None, ('shell', 'sky')), may hold values from 0 to 1
- inverse_error: float32 [32, 32, 128], P(None, ('shell', 'sky')), may hold values from 1 to 8
Outputs:
- extinction: float32 [512, 65536], P('shell', 'sky')
- sensitivity: float32 [512, 65536], P('shell', 'sky')
- residual: float32 [32, 32, 128], P(None, ('shell', 'sky'))
The draws below stay inside these ranges and needn't reach their ends.
Inputs may be any that keep to these rules, and one draw needn't show every extreme that they name: `star_count`: live slots from holder h to owner o. In every draw some owner gets 128 live slots from every holder; holders' loads differ.
All inputs are finite; a program needn't handle non-finite values.
Results may differ from the reference program's by a relative error of at most 0.00018.
Values sent between devices are 32-bit elements; how exact they have to be, the bound alone decides.
A program may use at most 128 MiB of HBM per device.

```python
import math
import jax
import jax.numpy as jnp

SHELL_DEV = 32
PIX_DEV = 32768
PASSES = 4
CAP = 128
SHELLS = 512
PIXELS = 65536
HOLDERS = 32
N_SKY = 2


def draw_star_count(key, part):
    first_key, second_key, third_key = jax.random.split(jax.random.fold_in(key, 17), 3)
    uniform_part = jax.random.randint(first_key, (HOLDERS, HOLDERS), 0, CAP + 1)
    holder_level = jax.random.randint(second_key, (HOLDERS, 1), 2, 5)
    counted = jnp.minimum(uniform_part * holder_level // 2, CAP)
    full_owner = jax.random.randint(third_key, (), 0, HOLDERS)
    owner_index = jnp.arange(HOLDERS, dtype=jnp.int32)[None, :]
    return jnp.where(owner_index == full_owner, CAP, counted).astype(jnp.int32)


def touch_ends(array, rng, low, largest):
    index_at = [jax.random.randint(jax.random.fold_in(rng, axis), (), 0, length) for axis, length in enumerate(array.shape)]
    widest = array.shape.index(max(array.shape))
    neighbour = index_at[:widest] + [(index_at[widest] + 1) % array.shape[widest]] + index_at[widest + 1:]
    return array.at[tuple(index_at)].set(low).at[tuple(neighbour)].set(largest)


def levels(stream_key, dims, shards, smallest, top_value):
    loudness, own = 1.0, jax.random.fold_in(stream_key, 6)
    for dim, blocks in shards:
        draws = jnp.exp(jax.random.uniform(jax.random.fold_in(own, dim), (blocks,), jnp.float32, smallest / len(shards), top_value / len(shards)))
        loudness = loudness * jnp.repeat(draws, dims[dim] // blocks).reshape([-1 if axis == dim else 1 for axis in range(len(dims))])
    return loudness


def normal_values(own_key, extent, width, limit, shards=(), kind=jnp.bfloat16):
    array = width * jax.random.normal(own_key, extent, jnp.float32)
    if shards:
        array = array * levels(own_key, extent, shards, -0.22, 0.18)
    return jnp.clip(array, -limit, limit).astype(kind)


def setup_inputs(seed: int = 0) -> dict:
    seeds = jax.random.split(jax.random.key(seed), 8)
    excitation = normal_values(seeds[0], (SHELLS, PIXELS), 0.3, 1.8, ((0, 16), (1, 2)), jnp.float32)
    star_shell = touch_ends(jax.random.randint(seeds[1], (HOLDERS, HOLDERS, CAP), 0, SHELL_DEV), jax.random.fold_in(seeds[1], 1), 0, SHELL_DEV - 1).astype(jnp.int32)
    star_pixel = touch_ends(jax.random.randint(seeds[2], (HOLDERS, HOLDERS, CAP), 0, PIX_DEV), jax.random.fold_in(seeds[2], 1), 0, PIX_DEV - 1).astype(jnp.int32)
    star_fraction = jnp.clip(1.0 * jax.random.uniform(seeds[3], (HOLDERS, HOLDERS, CAP), jnp.float32) ** levels(seeds[3], (HOLDERS, HOLDERS, CAP), ((0, 32),), -0.2, 0.2), 0.0, 1.0)
    star_count = draw_star_count(jax.random.fold_in(seeds[7], 71), 0)
    observed = jnp.clip(1.0 * jax.random.uniform(seeds[5], (HOLDERS, HOLDERS, CAP), jnp.float32) ** levels(seeds[5], (HOLDERS, HOLDERS, CAP), ((1, 32),), -0.2, 0.2), 0.0, 1.0)
    inverse_error = jnp.clip(jnp.exp(math.log(8.0) - 2.0794415 * jax.random.uniform(seeds[6], (HOLDERS, HOLDERS, CAP), jnp.float32) ** levels(seeds[6], (HOLDERS, HOLDERS, CAP), ((1, 32),), -0.2, 0.2)), 1.0, 8.0)
    return {"excitation": excitation, "star_shell": star_shell, "star_pixel": star_pixel, "star_fraction": star_fraction, "star_count": star_count, "observed": observed, "inverse_error": inverse_error}


depth_span = 2.0


def reference(excitation, star_shell, star_pixel, star_fraction, star_count, observed, inverse_error):
    shells_all = excitation.shape[0]
    pixels_all = excitation.shape[1]
    thickness = depth_span / shells_all
    logdens = excitation
    for sweep in range(PASSES):
        padded = jnp.pad(logdens, ((1, 1), (0, 0)))
        logdens = 0.3 * (padded[:-2] + padded[2:]) + 0.35 * logdens + excitation
    density = jnp.exp(logdens)
    extinction = jnp.cumsum(density * thickness, axis=0)
    holder = jnp.arange(HOLDERS, dtype=jnp.int32)
    shell_index = (holder // N_SKY)[:, None, None] * SHELL_DEV + star_shell
    pixel_index = (holder % N_SKY)[:, None, None] * PIX_DEV + star_pixel
    slot_index = (shell_index * pixels_all + pixel_index).astype(jnp.int32)
    slot_alive = jnp.arange(CAP, dtype=jnp.int32)[None, None, :] < star_count[:, :, None]
    near_share = 1.0 - star_fraction
    looked = extinction.reshape(-1)[slot_index] - near_share * thickness * density.reshape(-1)[slot_index]
    column = jnp.where(slot_alive, looked, 0.0)
    transmit = jnp.exp(-column)
    residual = jnp.where(slot_alive, (observed - (1.0 - transmit)) * inverse_error, 0.0)
    pull_back = -residual * inverse_error * transmit
    flat_index = slot_index.reshape(-1)
    impulse = jnp.zeros((shells_all * pixels_all,), excitation.dtype)
    impulse = impulse.at[flat_index].add(pull_back.reshape(-1)).reshape(shells_all, pixels_all)
    nearby = jnp.zeros((shells_all * pixels_all,), excitation.dtype)
    nearby = nearby.at[flat_index].add((near_share * pull_back).reshape(-1)).reshape(shells_all, pixels_all)
    tail_sums = jnp.flip(jnp.cumsum(jnp.flip(impulse, 0), axis=0), 0)
    sensitivity = density * (tail_sums - nearby)
    return extinction, sensitivity, residual
```

```python
import jax
import jax.numpy as jnp
import numpy as np
from jax import lax
from jax.experimental import pallas as pl
from jax.experimental.pallas import tpu as pltpu
from jax.sharding import PartitionSpec as P

PASSES = 4
LANES = 128
TILE = 2048

depth_span = 2.0


def split2(x):
    high = x.astype(jnp.bfloat16).astype(jnp.float32)
    return high, x - high


def stencil_matrix(rows, first, last):
    wide = rows + 2 * PASSES
    valid = np.ones((wide, 1))
    if first:
        valid[:PASSES] = 0.0
    if last:
        valid[-PASSES:] = 0.0
    eye = np.eye(wide)
    out = eye
    for _ in range(PASSES):
        padded = np.pad(out, ((1, 1), (0, 0)))
        out = valid * (0.3 * (padded[:-2] + padded[2:]) + 0.35 * out + eye)
    out = out[PASSES:-PASSES]
    local = out[:, PASSES:-PASSES]
    halo = np.concatenate([out[:, :PASSES], out[:, -PASSES:]], 1)
    return np.concatenate([local, local, halo, halo], 1).astype(np.float32)


def density_kernel(
    n_own, thickness, row_ref, lo_ref, mat_ref, tri_ref, exc_ref, bef_ref, aft_ref,
    dens_ref, pre_ref, sum_ref, base_ref, slope_ref, pre_tab, dens_tab, got,
):
    step = pl.program_id(0)
    rows, width = exc_ref.shape
    blocks = width // LANES
    e1, e2 = split2(exc_ref[...])
    h1, h2 = split2(jnp.concatenate([bef_ref[...], aft_ref[...]], 0))
    stacked = jnp.concatenate([e1, e2, h1, h2], 0).astype(jnp.bfloat16)
    both = jnp.dot(mat_ref[...], stacked, preferred_element_type=jnp.float32)
    dens = jnp.exp(both[:rows] + both[rows:])
    d1, d2 = split2(dens)
    pre = thickness * jnp.dot(
        tri_ref[...],
        jnp.concatenate([d1, d2], 0).astype(jnp.bfloat16),
        preferred_element_type=jnp.float32,
    )
    dens_ref[...] = dens
    pre_ref[...] = pre
    sum_ref[...] = pre[rows - 1 : rows]
    for b in range(blocks):
        at = pl.ds(pl.multiple_of((step * blocks + b) * rows, rows), rows)
        pre_tab[at, :] = pre[:, b * LANES : (b + 1) * LANES]
        dens_tab[at, :] = dens[:, b * LANES : (b + 1) * LANES]

    @pl.when(step == pl.num_programs(0) - 1)
    def _():
        lane = lax.broadcasted_iota(jnp.int32, (LANES, LANES), 1)
        sub = lax.broadcasted_iota(jnp.int32, (LANES, LANES), 0)

        def chunk(pair, carry):
            for k in range(2):
                o = pair * 2 + k
                for c in range(LANES):
                    at = row_ref[o, c]
                    got[k, c : c + 1, :] = pre_tab[pl.ds(at, 1), :]
                    got[k, LANES + c : LANES + c + 1, :] = dens_tab[pl.ds(at, 1), :]
            for k in range(2):
                o = pair * 2 + k
                hot = (sub == lo_ref[pl.ds(o, 1), :]).astype(jnp.bfloat16)
                g1, g2 = split2(got[k])
                picked = jnp.dot(
                    jnp.concatenate([g1, g2], 0).astype(jnp.bfloat16),
                    hot,
                    preferred_element_type=jnp.float32,
                )
                p = picked[:LANES] + picked[2 * LANES : 3 * LANES]
                d = picked[LANES : 2 * LANES] + picked[3 * LANES :]
                base_ref[pl.ds(o, 1), :] = jnp.sum(jnp.where(sub == lane, p, 0.0), 0, keepdims=True)
                slope_ref[pl.ds(o, 1), :] = jnp.sum(jnp.where(sub == lane, d, 0.0), 0, keepdims=True)
            return carry

        lax.fori_loop(0, n_own // 2, chunk, 0)


def column_kernel(n_own, thickness, hi_ref, lo_ref, share_ref, live_ref, base_ref, slope_ref, off_ref, col_ref):
    groups = off_ref.shape[0]
    o1, o2 = split2(off_ref[...])
    table = jnp.concatenate([o1.T, o2.T], 0).astype(jnp.bfloat16)
    tall = lax.broadcasted_iota(jnp.int32, (groups, LANES), 0)
    sub = lax.broadcasted_iota(jnp.int32, (LANES, LANES), 0)

    def chunk(o, carry):
        hot = (tall == hi_ref[pl.ds(o, 1), :]).astype(jnp.bfloat16)
        got = jnp.dot(table, hot, preferred_element_type=jnp.float32)
        got = got[:LANES] + got[LANES:]
        off = jnp.sum(jnp.where(sub == lo_ref[pl.ds(o, 1), :], got, 0.0), 0, keepdims=True)
        at = pl.ds(o, 1)
        col = base_ref[at, :] + off - share_ref[at, :] * thickness * slope_ref[at, :]
        col_ref[at, :] = jnp.where(live_ref[at, :] > 0, col, -1.0)
        return carry

    lax.fori_loop(0, n_own, chunk, 0)


GROUP = 8


def scatter_kernel(
    n_own, row_ref, rows_ref, lo_ref, share_ref, pull_ref, mat_ref,
    s_ref, tail_ref, imp_tab, near_tab, upd,
):
    step = pl.program_id(0)
    rows, width = s_ref.shape
    blocks = width // LANES

    @pl.when(step == 0)
    def _():
        total = imp_tab.shape[0]

        def clear(i, carry):
            at = pl.ds(pl.multiple_of(i * 256, 256), 256)
            imp_tab[at, :] = jnp.zeros((256, LANES), jnp.float32)
            near_tab[at, :] = jnp.zeros((256, LANES), jnp.float32)
            return carry

        lax.fori_loop(0, total // 256, clear, 0)
        sub = lax.broadcasted_iota(jnp.int32, (LANES, LANES), 0)
        lane = lax.broadcasted_iota(jnp.int32, (LANES, LANES), 1)
        grouped = sub // GROUP == lane // GROUP

        def chunk(o, carry):
            at = pl.ds(o, 1)
            same = jnp.broadcast_to(rows_ref[at, :], (LANES, LANES))
            same = jnp.logical_and(same == same.T, grouped)
            pull = pull_ref[at, :]
            a1, a2 = split2(jnp.where(same, pull, 0.0))
            b1, b2 = split2(jnp.where(same, pull * share_ref[at, :], 0.0))
            hot = (sub == lo_ref[at, :]).astype(jnp.bfloat16)
            out = lax.dot_general(
                jnp.concatenate([a1, a2, b1, b2], 0).astype(jnp.bfloat16),
                hot,
                (((1,), (1,)), ((), ())),
                preferred_element_type=jnp.float32,
            )
            upd[:LANES] = out[:LANES] + out[LANES : 2 * LANES]
            upd[LANES:] = out[2 * LANES : 3 * LANES] + out[3 * LANES :]
            for g in range(LANES // GROUP):
                cs = range(g * GROUP, (g + 1) * GROUP)
                where = [row_ref[o, c] for c in cs]
                imps = [imp_tab[pl.ds(w, 1), :] + upd[c : c + 1, :] for w, c in zip(where, cs)]
                nears = [near_tab[pl.ds(w, 1), :] + upd[LANES + c : LANES + c + 1, :] for w, c in zip(where, cs)]
                for w, a, b in zip(where, imps, nears):
                    imp_tab[pl.ds(w, 1), :] = a
                    near_tab[pl.ds(w, 1), :] = b
            return carry

        lax.fori_loop(0, n_own, chunk, 0)

    def natural(tab):
        parts = []
        for b in range(blocks):
            at = pl.ds(pl.multiple_of((step * blocks + b) * rows, rows), rows)
            parts.append(tab[at, :])
        return jnp.concatenate(parts, 1)

    i1, i2 = split2(natural(imp_tab))
    n1, n2 = split2(natural(near_tab))
    out = jnp.dot(
        mat_ref[...],
        jnp.concatenate([i1, i2, n1, n2], 0).astype(jnp.bfloat16),
        preferred_element_type=jnp.float32,
    )
    s_ref[...] = out[:rows]
    tail_ref[...] = out[rows : rows + 1]


def exchange(blocks, size, upper):
    ids = np.arange(size)
    strict = (ids[:, None] < ids[None, :]) if upper else (ids[:, None] > ids[None, :])
    spread = blocks.reshape(size, -1)
    got = lax.all_to_all(spread, "shell", split_axis=0, concat_axis=0, tiled=True)
    summed = jnp.dot(
        jnp.asarray(strict, jnp.float32), got,
        precision=lax.Precision.HIGHEST, preferred_element_type=jnp.float32,
    )
    return lax.all_to_all(summed, "shell", split_axis=0, concat_axis=0, tiled=True)


def body(excitation, star_shell, star_pixel, star_fraction, star_count, observed, inverse_error):
    rows, cols = excitation.shape
    size = lax.axis_size("shell")
    me = lax.axis_index("shell")
    thickness = depth_span / (rows * size)
    n_own = star_shell.shape[1]
    groups = cols // LANES
    tile = min(TILE, cols)
    f32, bf16 = jnp.float32, jnp.bfloat16

    up = [(i, i + 1) for i in range(size - 1)]
    down = [(i + 1, i) for i in range(size - 1)]
    before = lax.ppermute(excitation[-PASSES:], "shell", up)
    after = lax.ppermute(excitation[:PASSES], "shell", down)

    pixel = star_pixel[0]
    hi, lo = pixel // LANES, pixel % LANES
    row = hi * rows + star_shell[0]
    share = 1.0 - star_fraction[0]
    live = (jnp.arange(LANES, dtype=jnp.int32)[None, :] < star_count[0][:, None]).astype(jnp.int32)

    mats = np.stack([stencil_matrix(rows, a, b) for a, b in ((0, 0), (1, 0), (0, 1), (1, 1))])
    top = mats.astype(bf16)
    rest = (mats - top.astype(np.float32)).astype(bf16)
    which = (me == 0).astype(jnp.int32) + 2 * (me == size - 1).astype(jnp.int32)
    mat = lax.dynamic_index_in_dim(jnp.asarray(np.concatenate([top, rest], 1)), which, 0, False)
    tri = np.tril(np.ones((rows, rows), np.float32))
    tri2 = jnp.asarray(np.concatenate([tri, tri], 1).astype(bf16))

    smem = pl.BlockSpec(memory_space=pltpu.SMEM)
    vmem = pl.BlockSpec(memory_space=pltpu.VMEM)
    full = lambda shape: pl.BlockSpec(shape, lambda i: (0, 0))
    cut = lambda r: pl.BlockSpec((r, tile), lambda i: (0, i))
    stars = jax.ShapeDtypeStruct((n_own, LANES), f32)
    grid_shape = jax.ShapeDtypeStruct((rows, cols), f32)
    line = jax.ShapeDtypeStruct((1, cols), f32)
    limit = pltpu.CompilerParams(vmem_limit_bytes=48 * 2**20)

    density, prefix, sums, base, slope = pl.pallas_call(
        lambda *refs: density_kernel(n_own, thickness, *refs),
        grid=(cols // tile,),
        in_specs=[smem, full((n_own, LANES)), full(mat.shape), full(tri2.shape), cut(rows), cut(PASSES), cut(PASSES)],
        out_specs=[cut(rows), cut(rows), cut(1), full((n_own, LANES)), full((n_own, LANES))],
        out_shape=[grid_shape, grid_shape, line, stars, stars],
        scratch_shapes=[
            pltpu.VMEM((groups * rows, LANES), f32),
            pltpu.VMEM((groups * rows, LANES), f32),
            pltpu.VMEM((2, 2 * LANES, LANES), f32),
        ],
        compiler_params=limit,
        name="density",
    )(row, lo, mat, tri2, excitation, before, after)

    offset = exchange(sums, size, False)

    column = pl.pallas_call(
        lambda *refs: column_kernel(n_own, thickness, *refs),
        in_specs=[vmem] * 7,
        out_specs=vmem,
        out_shape=stars,
        compiler_params=limit,
        name="column",
    )(hi, lo, share, live, base, slope, offset.reshape(groups, LANES))

    both = ("shell", "sky")
    owned = lax.all_to_all(column[None], both, split_axis=1, concat_axis=0, tiled=True)
    transmit = jnp.exp(-owned)
    residual = jnp.where(owned > -0.5, (observed - (1.0 - transmit)) * inverse_error, 0.0)
    pull = jnp.where(owned > -0.5, -residual * inverse_error * transmit, 0.0)
    returned = lax.all_to_all(pull, both, split_axis=0, concat_axis=1, tiled=True)[0]

    upper = np.triu(np.ones((rows, rows), np.float32))
    eye = np.eye(rows, dtype=np.float32)
    top_row = np.zeros((16, 4 * rows), np.float32)
    top_row[0, : 2 * rows] = 1.0
    smat = jnp.asarray(
        np.concatenate([np.concatenate([upper, upper, -eye, -eye], 1), top_row], 0).astype(bf16)
    )
    local_sens, tails = pl.pallas_call(
        lambda *refs: scatter_kernel(n_own, *refs),
        grid=(cols // tile,),
        in_specs=[smem] + [full((n_own, LANES))] * 4 + [full(smat.shape)],
        out_specs=[cut(rows), cut(1)],
        out_shape=[grid_shape, line],
        scratch_shapes=[
            pltpu.VMEM((groups * rows, LANES), f32),
            pltpu.VMEM((groups * rows, LANES), f32),
            pltpu.VMEM((2 * LANES, LANES), f32),
        ],
        compiler_params=limit,
        name="scatter",
    )(row, row.astype(f32), lo, share, returned, smat)

    tail_offset = exchange(tails, size, True)
    extinction = prefix + offset.reshape(1, -1)
    sensitivity = density * (local_sens + tail_offset.reshape(1, -1))
    return extinction, sensitivity, residual


def solution(mesh):
    stars = P(("shell", "sky"), None, None)
    owners = P(None, ("shell", "sky"), None)
    return jax.shard_map(
        body,
        mesh=mesh,
        in_specs=(P("shell", "sky"), stars, stars, stars, P(("shell", "sky"), None), owners, owners),
        out_specs=(P("shell", "sky"), P("shell", "sky"), owners),
        check_vma=False,
    )
```

```python
import jax
import jax.numpy as jnp
import numpy as np
from jax import lax
from jax.experimental import pallas as pl
from jax.experimental.pallas import tpu as pltpu
from jax.sharding import PartitionSpec as P

PASSES = 4
LANES = 128
TILE = 2048

depth_span = 2.0


def split2(x):
    high = x.astype(jnp.bfloat16).astype(jnp.float32)
    return high, x - high


def stencil_matrix(rows, first, last):
    wide = rows + 2 * PASSES
    valid = np.ones((wide, 1))
    if first:
        valid[:PASSES] = 0.0
    if last:
        valid[-PASSES:] = 0.0
    eye = np.eye(wide)
    out = eye
    for _ in range(PASSES):
        padded = np.pad(out, ((1, 1), (0, 0)))
        out = valid * (0.3 * (padded[:-2] + padded[2:]) + 0.35 * out + eye)
    out = out[PASSES:-PASSES]
    local = out[:, PASSES:-PASSES]
    halo = np.concatenate([out[:, :PASSES], out[:, -PASSES:]], 1)
    return np.concatenate([local, local, halo, halo], 1).astype(np.float32)


def density_kernel(
    n_own, thickness, row_ref, lo_ref, mat_ref, tri_ref, exc_ref, bef_ref, aft_ref,
    dens_ref, pre_ref, sum_ref, base_ref, slope_ref, pre_tab, dens_tab, got,
):
    step = pl.program_id(0)
    rows, width = exc_ref.shape
    blocks = width // LANES
    e1, e2 = split2(exc_ref[...])
    h1, h2 = split2(jnp.concatenate([bef_ref[...], aft_ref[...]], 0))
    stacked = jnp.concatenate([e1, e2, h1, h2], 0).astype(jnp.bfloat16)
    both = jnp.dot(mat_ref[...], stacked, preferred_element_type=jnp.float32)
    dens = jnp.exp(both[:rows] + both[rows:])
    d1, d2 = split2(dens)
    pre = thickness * jnp.dot(
        tri_ref[...],
        jnp.concatenate([d1, d2], 0).astype(jnp.bfloat16),
        preferred_element_type=jnp.float32,
    )
    dens_ref[...] = dens
    pre_ref[...] = pre
    sum_ref[...] = pre[rows - 1 : rows]
    for b in range(blocks):
        at = pl.ds(pl.multiple_of((step * blocks + b) * rows, rows), rows)
        pre_tab[at, :] = pre[:, b * LANES : (b + 1) * LANES]
        dens_tab[at, :] = dens[:, b * LANES : (b + 1) * LANES]

    @pl.when(step == pl.num_programs(0) - 1)
    def _():
        lane = lax.broadcasted_iota(jnp.int32, (LANES, LANES), 1)
        sub = lax.broadcasted_iota(jnp.int32, (LANES, LANES), 0)

        def chunk(pair, carry):
            for k in range(2):
                o = pair * 2 + k
                for c in range(LANES):
                    at = row_ref[o, c]
                    got[k, c : c + 1, :] = pre_tab[pl.ds(at, 1), :]
                    got[k, LANES + c : LANES + c + 1, :] = dens_tab[pl.ds(at, 1), :]
            for k in range(2):
                o = pair * 2 + k
                hot = (sub == lo_ref[pl.ds(o, 1), :]).astype(jnp.bfloat16)
                g1, g2 = split2(got[k])
                picked = jnp.dot(
                    jnp.concatenate([g1, g2], 0).astype(jnp.bfloat16),
                    hot,
                    preferred_element_type=jnp.float32,
                )
                p = picked[:LANES] + picked[2 * LANES : 3 * LANES]
                d = picked[LANES : 2 * LANES] + picked[3 * LANES :]
                base_ref[pl.ds(o, 1), :] = jnp.sum(jnp.where(sub == lane, p, 0.0), 0, keepdims=True)
                slope_ref[pl.ds(o, 1), :] = jnp.sum(jnp.where(sub == lane, d, 0.0), 0, keepdims=True)
            return carry

        lax.fori_loop(0, n_own // 2, chunk, 0)


def others(count, me, act):
    def step(k, carry):
        act(lax.rem(me + k, count))
        return carry

    lax.fori_loop(1, count, step, 0)


def shell_exchange(n, me, upper, src, got, summed, out, sems):
    send1, recv1, send2, recv2 = sems

    def move(frm, to, send, recv, peer):
        return pltpu.make_async_remote_copy(
            src_ref=frm.at[peer], dst_ref=to.at[me], send_sem=send.at[peer], recv_sem=recv.at[me],
            device_id={"shell": peer}, device_id_type=pl.DeviceIdType.MESH,
        )

    def landed(frm, to, send, recv, peer):
        return pltpu.make_async_remote_copy(
            src_ref=frm.at[peer], dst_ref=to.at[peer], send_sem=send.at[peer], recv_sem=recv.at[peer],
            device_id={"shell": peer}, device_id_type=pl.DeviceIdType.MESH,
        )

    others(n, me, lambda p: move(src, got, send1, recv1, p).start())
    got[pl.ds(me, 1)] = src[pl.ds(me, 1)]
    others(n, me, lambda p: landed(src, got, send1, recv1, p).wait_recv())
    total = jnp.zeros(got.shape[1:], jnp.float32)
    for i in range(n):
        i = n - 1 - i if upper else i
        summed[i] = total
        total = total + got[i]
    others(n, me, lambda p: move(summed, out, send2, recv2, p).start())
    out[pl.ds(me, 1)] = summed[pl.ds(me, 1)]
    others(n, me, lambda p: landed(summed, out, send2, recv2, p).wait_recv())
    others(n, me, lambda p: move(src, got, send1, recv1, p).wait_send())
    others(n, me, lambda p: move(summed, out, send2, recv2, p).wait_send())


def tail_kernel(n, src, out, got, summed, *sems):
    me = lax.axis_index("shell")
    barrier = pltpu.get_barrier_semaphore()
    others(n, me, lambda p: pl.semaphore_signal(
        barrier, inc=1, device_id={"shell": p}, device_id_type=pl.DeviceIdType.MESH))
    pl.semaphore_wait(barrier, n - 1)
    shell_exchange(n, me, True, src, got, summed, out, sems)


def middle_kernel(
    n, n_sky, thickness, src, hi_ref, lo_ref, share_ref, live_ref, base_ref, slope_ref, obs_ref, inv_ref,
    off_out, res_ref, back_ref, got, summed, col, owned, pull, *sems,
):
    shell = lax.axis_index("shell")
    me = shell * n_sky + lax.axis_index("sky")
    n_all = n * n_sky
    where = lambda p: {"shell": p // n_sky, "sky": lax.rem(p, n_sky)}
    barrier = pltpu.get_barrier_semaphore()
    others(n_all, me, lambda p: pl.semaphore_signal(
        barrier, inc=1, device_id=where(p), device_id_type=pl.DeviceIdType.MESH))
    pl.semaphore_wait(barrier, n_all - 1)
    shell_exchange(n, shell, False, src, got, summed, off_out, sems[:4])

    groups = n * src.shape[1]
    o1, o2 = split2(off_out[...].reshape(groups, LANES))
    table = jnp.concatenate([o1.T, o2.T], 0).astype(jnp.bfloat16)
    tall = lax.broadcasted_iota(jnp.int32, (groups, LANES), 0)
    sub = lax.broadcasted_iota(jnp.int32, (LANES, LANES), 0)

    def chunk(quad, carry):
        for k in range(4):
            o = quad * 4 + k
            at = pl.ds(o, 1)
            hot = (tall == hi_ref[at, :]).astype(jnp.bfloat16)
            off = jnp.dot(table, hot, preferred_element_type=jnp.float32)
            off = off[:LANES] + off[LANES:]
            off = jnp.sum(jnp.where(sub == lo_ref[at, :], off, 0.0), 0, keepdims=True)
            value = base_ref[at, :] + off - share_ref[at, :] * thickness * slope_ref[at, :]
            col[o] = jnp.where(live_ref[at, :] > 0, value, -1.0)
        return carry

    lax.fori_loop(0, n_all // 4, chunk, 0)

    def move(frm, to, send, recv, peer, slot):
        return pltpu.make_async_remote_copy(
            src_ref=frm.at[peer], dst_ref=to.at[slot], send_sem=send.at[peer], recv_sem=recv.at[slot],
            device_id=where(peer), device_id_type=pl.DeviceIdType.MESH,
        )

    send3, recv3, send4, recv4 = sems[4:]
    others(n_all, me, lambda p: move(col, owned, send3, recv3, p, me).start())
    owned[pl.ds(me, 1)] = col[pl.ds(me, 1)]
    others(n_all, me, lambda p: move(col, owned, send3, recv3, p, p).wait_recv())
    column = owned[...]
    transmit = jnp.exp(-column)
    inverse = inv_ref[...]
    residual = jnp.where(column > -0.5, (obs_ref[...] - (1.0 - transmit)) * inverse, 0.0)
    res_ref[...] = residual
    pull[...] = jnp.where(column > -0.5, -residual * inverse * transmit, 0.0)
    others(n_all, me, lambda p: move(pull, back_ref, send4, recv4, p, me).start())
    back_ref[pl.ds(me, 1)] = pull[pl.ds(me, 1)]
    others(n_all, me, lambda p: move(pull, back_ref, send4, recv4, p, p).wait_recv())
    others(n_all, me, lambda p: move(col, owned, send3, recv3, p, me).wait_send())
    others(n_all, me, lambda p: move(pull, back_ref, send4, recv4, p, me).wait_send())


GROUP = 8


def scatter_kernel(
    n_own, row_ref, rows_ref, lo_ref, share_ref, pull_ref, mat_ref, pre_ref, off_ref,
    s_ref, tail_ref, ext_ref, imp_tab, near_tab, upd,
):
    step = pl.program_id(0)
    rows, width = s_ref.shape
    blocks = width // LANES

    @pl.when(step == 0)
    def _():
        total = imp_tab.shape[0]

        def clear(i, carry):
            at = pl.ds(pl.multiple_of(i * 256, 256), 256)
            imp_tab[at, :] = jnp.zeros((256, LANES), jnp.float32)
            near_tab[at, :] = jnp.zeros((256, LANES), jnp.float32)
            return carry

        lax.fori_loop(0, total // 256, clear, 0)
        sub = lax.broadcasted_iota(jnp.int32, (LANES, LANES), 0)
        lane = lax.broadcasted_iota(jnp.int32, (LANES, LANES), 1)
        grouped = sub // GROUP == lane // GROUP

        def chunk(o, carry):
            at = pl.ds(o, 1)
            same = jnp.broadcast_to(rows_ref[at, :], (LANES, LANES))
            same = jnp.logical_and(same == same.T, grouped)
            pull = pull_ref[o]
            a1, a2 = split2(jnp.where(same, pull, 0.0))
            b1, b2 = split2(jnp.where(same, pull * share_ref[at, :], 0.0))
            hot = (sub == lo_ref[at, :]).astype(jnp.bfloat16)
            out = lax.dot_general(
                jnp.concatenate([a1, a2, b1, b2], 0).astype(jnp.bfloat16),
                hot,
                (((1,), (1,)), ((), ())),
                preferred_element_type=jnp.float32,
            )
            upd[:LANES] = out[:LANES] + out[LANES : 2 * LANES]
            upd[LANES:] = out[2 * LANES : 3 * LANES] + out[3 * LANES :]
            for g in range(LANES // GROUP):
                cs = range(g * GROUP, (g + 1) * GROUP)
                where = [row_ref[o, c] for c in cs]
                imps = [imp_tab[pl.ds(w, 1), :] + upd[c : c + 1, :] for w, c in zip(where, cs)]
                nears = [near_tab[pl.ds(w, 1), :] + upd[LANES + c : LANES + c + 1, :] for w, c in zip(where, cs)]
                for w, a, b in zip(where, imps, nears):
                    imp_tab[pl.ds(w, 1), :] = a
                    near_tab[pl.ds(w, 1), :] = b
            return carry

        lax.fori_loop(0, n_own, chunk, 0)

    def natural(tab):
        parts = []
        for b in range(blocks):
            at = pl.ds(pl.multiple_of((step * blocks + b) * rows, rows), rows)
            parts.append(tab[at, :])
        return jnp.concatenate(parts, 1)

    i1, i2 = split2(natural(imp_tab))
    n1, n2 = split2(natural(near_tab))
    out = jnp.dot(
        mat_ref[...],
        jnp.concatenate([i1, i2, n1, n2], 0).astype(jnp.bfloat16),
        preferred_element_type=jnp.float32,
    )
    s_ref[...] = out[:rows]
    tail_ref[...] = out[rows : rows + 1]
    ext_ref[...] = pre_ref[...] + off_ref[...]


def body(excitation, star_shell, star_pixel, star_fraction, star_count, observed, inverse_error):
    rows, cols = excitation.shape
    size = lax.axis_size("shell")
    me = lax.axis_index("shell")
    thickness = depth_span / (rows * size)
    n_own = star_shell.shape[1]
    groups = cols // LANES
    tile = min(TILE, cols)
    f32, bf16 = jnp.float32, jnp.bfloat16

    up = [(i, i + 1) for i in range(size - 1)]
    down = [(i + 1, i) for i in range(size - 1)]
    before = lax.ppermute(excitation[-PASSES:], "shell", up)
    after = lax.ppermute(excitation[:PASSES], "shell", down)

    pixel = star_pixel[0]
    hi, lo = pixel // LANES, pixel % LANES
    row = hi * rows + star_shell[0]
    share = 1.0 - star_fraction[0]
    live = (jnp.arange(LANES, dtype=jnp.int32)[None, :] < star_count[0][:, None]).astype(jnp.int32)

    mats = np.stack([stencil_matrix(rows, a, b) for a, b in ((0, 0), (1, 0), (0, 1), (1, 1))])
    top = mats.astype(bf16)
    rest = (mats - top.astype(np.float32)).astype(bf16)
    which = (me == 0).astype(jnp.int32) + 2 * (me == size - 1).astype(jnp.int32)
    mat = lax.dynamic_index_in_dim(jnp.asarray(np.concatenate([top, rest], 1)), which, 0, False)
    tri = np.tril(np.ones((rows, rows), np.float32))
    tri2 = jnp.asarray(np.concatenate([tri, tri], 1).astype(bf16))

    smem = pl.BlockSpec(memory_space=pltpu.SMEM)
    vmem = pl.BlockSpec(memory_space=pltpu.VMEM)
    full = lambda shape: pl.BlockSpec(shape, lambda i: (0, 0))
    cut = lambda r: pl.BlockSpec((r, tile), lambda i: (0, i))
    stars = jax.ShapeDtypeStruct((n_own, LANES), f32)
    grid_shape = jax.ShapeDtypeStruct((rows, cols), f32)
    line = jax.ShapeDtypeStruct((1, cols), f32)
    limit = pltpu.CompilerParams(vmem_limit_bytes=48 * 2**20)

    density, prefix, sums, base, slope = pl.pallas_call(
        lambda *refs: density_kernel(n_own, thickness, *refs),
        grid=(cols // tile,),
        in_specs=[smem, full((n_own, LANES)), full(mat.shape), full(tri2.shape), cut(rows), cut(PASSES), cut(PASSES)],
        out_specs=[cut(rows), cut(rows), cut(1), full((n_own, LANES)), full((n_own, LANES))],
        out_shape=[grid_shape, grid_shape, line, stars, stars],
        scratch_shapes=[
            pltpu.VMEM((groups * rows, LANES), f32),
            pltpu.VMEM((groups * rows, LANES), f32),
            pltpu.VMEM((2, 2 * LANES, LANES), f32),
        ],
        compiler_params=limit,
        name="density",
    )(row, lo, mat, tri2, excitation, before, after)

    n_sky = lax.axis_size("sky")
    n_all = size * n_sky
    spread = (size, groups // size, LANES)
    blocks = jax.ShapeDtypeStruct(spread, f32)
    slots = jax.ShapeDtypeStruct((n_all, 1, LANES), f32)
    hold = lambda like: pltpu.VMEM(like.shape, f32)
    dma = lambda k: pltpu.SemaphoreType.DMA((k,))

    def remote(number):
        return pltpu.CompilerParams(
            collective_id=number, has_side_effects=True, vmem_limit_bytes=48 * 2**20
        )

    offset, residual, returned = pl.pallas_call(
        lambda *refs: middle_kernel(size, n_sky, thickness, *refs),
        in_specs=[vmem] * 9,
        out_specs=[vmem] * 3,
        out_shape=[blocks, slots, slots],
        scratch_shapes=[hold(blocks), hold(blocks), hold(slots), hold(slots), hold(slots)]
        + [dma(size)] * 4 + [dma(n_all)] * 4,
        compiler_params=remote(0),
        name="middle",
    )(sums.reshape(spread), hi, lo, share, live, base, slope, observed, inverse_error)

    upper = np.triu(np.ones((rows, rows), np.float32))
    eye = np.eye(rows, dtype=np.float32)
    top_row = np.zeros((16, 4 * rows), np.float32)
    top_row[0, : 2 * rows] = 1.0
    smat = jnp.asarray(
        np.concatenate([np.concatenate([upper, upper, -eye, -eye], 1), top_row], 0).astype(bf16)
    )
    local_sens, tails, extinction = pl.pallas_call(
        lambda *refs: scatter_kernel(n_own, *refs),
        grid=(cols // tile,),
        in_specs=[smem] + [full((n_own, LANES))] * 3
        + [pl.BlockSpec((n_own, 1, LANES), lambda i: (0, 0, 0)), full(smat.shape), cut(rows), cut(1)],
        out_specs=[cut(rows), cut(1), cut(rows)],
        out_shape=[grid_shape, line, grid_shape],
        scratch_shapes=[
            pltpu.VMEM((groups * rows, LANES), f32),
            pltpu.VMEM((groups * rows, LANES), f32),
            pltpu.VMEM((2 * LANES, LANES), f32),
        ],
        compiler_params=limit,
        name="scatter",
    )(row, row.astype(f32), lo, share, returned, smat, prefix, offset.reshape(1, -1))

    tail_offset = pl.pallas_call(
        lambda *refs: tail_kernel(size, *refs),
        in_specs=[vmem],
        out_specs=vmem,
        out_shape=blocks,
        scratch_shapes=[hold(blocks), hold(blocks)] + [dma(size)] * 4,
        compiler_params=remote(1),
        name="tails",
    )(tails.reshape(spread))
    sensitivity = density * (local_sens + tail_offset.reshape(1, -1))
    return extinction, sensitivity, residual


def solution(mesh):
    stars = P(("shell", "sky"), None, None)
    owners = P(None, ("shell", "sky"), None)
    return jax.shard_map(
        body,
        mesh=mesh,
        in_specs=(P("shell", "sky"), stars, stars, stars, P(("shell", "sky"), None), owners, owners),
        out_specs=(P("shell", "sky"), P("shell", "sky"), owners),
        check_vma=False,
    )
```

```python
import jax
import jax.numpy as jnp
import numpy as np
from jax import lax
from jax.experimental import pallas as pl
from jax.experimental.pallas import tpu as pltpu
from jax.sharding import PartitionSpec as P

PASSES = 4
LANES = 128
TILE = 2048

depth_span = 2.0


def split2(x):
    high = x.astype(jnp.bfloat16).astype(jnp.float32)
    return high, x - high


def stencil_matrix(rows, first, last):
    wide = rows + 2 * PASSES
    valid = np.ones((wide, 1))
    if first:
        valid[:PASSES] = 0.0
    if last:
        valid[-PASSES:] = 0.0
    eye = np.eye(wide)
    out = eye
    for _ in range(PASSES):
        padded = np.pad(out, ((1, 1), (0, 0)))
        out = valid * (0.3 * (padded[:-2] + padded[2:]) + 0.35 * out + eye)
    out = out[PASSES:-PASSES]
    local = out[:, PASSES:-PASSES]
    halo = np.concatenate([out[:, :PASSES], out[:, -PASSES:]], 1)
    return np.concatenate([local, local, halo, halo], 1).astype(np.float32)


def others(count, me, act):
    def step(k, carry):
        act(lax.rem(me + k, count))
        return carry

    lax.fori_loop(1, count, step, 0)


def shell_exchange(n, me, upper, src, got, summed, out, sems, meanwhile=lambda half: None):
    send1, recv1, send2, recv2 = sems

    def move(frm, to, send, recv, peer, slot):
        return pltpu.make_async_remote_copy(
            src_ref=frm.at[peer], dst_ref=to.at[slot], send_sem=send.at[peer], recv_sem=recv.at[slot],
            device_id={"shell": peer}, device_id_type=pl.DeviceIdType.MESH,
        )

    others(n, me, lambda p: move(src, got, send1, recv1, p, me).start())
    got[pl.ds(me, 1)] = src[pl.ds(me, 1)]
    meanwhile(0)
    others(n, me, lambda p: move(src, got, send1, recv1, p, p).wait_recv())
    total = jnp.zeros(got.shape[1:], jnp.float32)
    for i in range(n):
        i = n - 1 - i if upper else i
        summed[i] = total
        total = total + got[i]
    others(n, me, lambda p: move(summed, out, send2, recv2, p, me).start())
    out[pl.ds(me, 1)] = summed[pl.ds(me, 1)]
    meanwhile(1)
    others(n, me, lambda p: move(summed, out, send2, recv2, p, p).wait_recv())
    others(n, me, lambda p: move(src, got, send1, recv1, p, me).wait_send())
    others(n, me, lambda p: move(summed, out, send2, recv2, p, me).wait_send())


def tail_kernel(n, src, out, got, summed, *sems):
    me = lax.axis_index("shell")
    barrier = pltpu.get_barrier_semaphore()
    others(n, me, lambda p: pl.semaphore_signal(
        barrier, inc=1, device_id={"shell": p}, device_id_type=pl.DeviceIdType.MESH))
    pl.semaphore_wait(barrier, n - 1)
    shell_exchange(n, me, True, src, got, summed, out, sems)


def field_kernel(
    n, n_sky, thickness, row_ref, exc_ref, mat_ref, tri_ref, hi_ref, lo_ref, share_ref, live_ref, obs_ref, inv_ref,
    dens_out, pre_out, off_out, res_ref, back_ref,
    last4, first4, before, after, dens_nat, pre_nat, pre_tab, dens_tab, got_rows, base_ref, slope_ref,
    src, got, summed, col, owned, pull, out_sems, up_send, up_recv, down_send, down_recv, *sems,
):
    shell = lax.axis_index("shell")
    me = shell * n_sky + lax.axis_index("sky")
    n_all = n * n_sky
    rows, cols = exc_ref.shape
    tiles, _, width = last4.shape
    blocks = width // LANES
    part = src.shape[1]
    where = lambda p: {"shell": p // n_sky, "sky": lax.rem(p, n_sky)}
    barrier = pltpu.get_barrier_semaphore()
    others(n_all, me, lambda p: pl.semaphore_signal(
        barrier, inc=1, device_id=where(p), device_id_type=pl.DeviceIdType.MESH))
    for t in range(tiles):
        at = slice(t * width, (t + 1) * width)
        last4[t] = exc_ref[rows - PASSES :, at]
        first4[t] = exc_ref[:PASSES, at]

    @pl.when(shell == 0)
    def _():
        before[...] = jnp.zeros(before.shape, jnp.float32)

    @pl.when(shell == n - 1)
    def _():
        after[...] = jnp.zeros(after.shape, jnp.float32)

    pl.semaphore_wait(barrier, n_all - 1)

    def upward(t):
        return pltpu.make_async_remote_copy(
            src_ref=last4.at[t], dst_ref=before.at[t], send_sem=up_send.at[t], recv_sem=up_recv.at[t],
            device_id={"shell": lax.rem(shell + 1, n)}, device_id_type=pl.DeviceIdType.MESH,
        )

    def downward(t):
        return pltpu.make_async_remote_copy(
            src_ref=first4.at[t], dst_ref=after.at[t], send_sem=down_send.at[t], recv_sem=down_recv.at[t],
            device_id={"shell": lax.rem(shell + n - 1, n)}, device_id_type=pl.DeviceIdType.MESH,
        )

    has_up, has_down = shell < n - 1, shell > 0

    def send(t, carry):
        pl.when(has_up)(lambda: upward(t).start())
        pl.when(has_down)(lambda: downward(t).start())
        return carry

    lax.fori_loop(0, tiles, send, 0)

    def outward(t):
        at = pl.ds(pl.multiple_of(t * width, width), width)
        return (
            pltpu.make_async_copy(dens_nat.at[t], dens_out.at[:, at], out_sems.at[0, t]),
            pltpu.make_async_copy(pre_nat.at[t], pre_out.at[:, at], out_sems.at[1, t]),
        )

    def tile(t, carry):
        pl.when(has_down)(lambda: upward(t).wait_recv())
        pl.when(has_up)(lambda: downward(t).wait_recv())
        e1, e2 = split2(exc_ref[:, pl.ds(pl.multiple_of(t * width, width), width)])
        h1, h2 = split2(jnp.concatenate([before[t], after[t]], 0))
        stacked = jnp.concatenate([e1, e2, h1, h2], 0).astype(jnp.bfloat16)
        both = jnp.dot(mat_ref[...], stacked, preferred_element_type=jnp.float32)
        dens = jnp.exp(both[:rows] + both[rows:])
        d1, d2 = split2(dens)
        pre = thickness * jnp.dot(
            tri_ref[...],
            jnp.concatenate([d1, d2], 0).astype(jnp.bfloat16),
            preferred_element_type=jnp.float32,
        )
        dens_nat[t] = dens
        pre_nat[t] = pre
        for b in range(blocks):
            g = t * blocks + b
            at = pl.ds(pl.multiple_of(g * rows, rows), rows)
            pre_tab[at, :] = pre[:, b * LANES : (b + 1) * LANES]
            dens_tab[at, :] = dens[:, b * LANES : (b + 1) * LANES]
            src[g // part, pl.ds(lax.rem(g, part), 1), :] = pre[rows - 1 :, b * LANES : (b + 1) * LANES]
        for copy in outward(t):
            copy.start()
        return carry

    lax.fori_loop(0, tiles, tile, 0)
    lane = lax.broadcasted_iota(jnp.int32, (LANES, LANES), 1)
    sub = lax.broadcasted_iota(jnp.int32, (LANES, LANES), 0)

    def pick(pair, carry):
        for k in range(2):
            o = pair * 2 + k
            for c in range(LANES):
                at = row_ref[o, c]
                got_rows[k, c : c + 1, :] = pre_tab[pl.ds(at, 1), :]
                got_rows[k, LANES + c : LANES + c + 1, :] = dens_tab[pl.ds(at, 1), :]
        for k in range(2):
            o = pair * 2 + k
            hot = (sub == lo_ref[pl.ds(o, 1), :]).astype(jnp.bfloat16)
            g1, g2 = split2(got_rows[k])
            picked = jnp.dot(
                jnp.concatenate([g1, g2], 0).astype(jnp.bfloat16),
                hot,
                preferred_element_type=jnp.float32,
            )
            p = picked[:LANES] + picked[2 * LANES : 3 * LANES]
            d = picked[LANES : 2 * LANES] + picked[3 * LANES :]
            base_ref[pl.ds(o, 1), :] = jnp.sum(jnp.where(sub == lane, p, 0.0), 0, keepdims=True)
            slope_ref[pl.ds(o, 1), :] = jnp.sum(jnp.where(sub == lane, d, 0.0), 0, keepdims=True)
        return carry

    pairs = n_all // 2
    cut = [0, pairs // 2, pairs]
    shell_exchange(
        n, shell, False, src, got, summed, off_out, sems[:4],
        lambda half: lax.fori_loop(cut[half], cut[half + 1], pick, 0),
    )

    groups = n * src.shape[1]
    o1, o2 = split2(off_out[...].reshape(groups, LANES))
    table = jnp.concatenate([o1.T, o2.T], 0).astype(jnp.bfloat16)
    tall = lax.broadcasted_iota(jnp.int32, (groups, LANES), 0)

    def chunk(quad, carry):
        for k in range(4):
            o = quad * 4 + k
            at = pl.ds(o, 1)
            hot = (tall == hi_ref[at, :]).astype(jnp.bfloat16)
            off = jnp.dot(table, hot, preferred_element_type=jnp.float32)
            off = off[:LANES] + off[LANES:]
            off = jnp.sum(jnp.where(sub == lo_ref[at, :], off, 0.0), 0, keepdims=True)
            value = base_ref[at, :] + off - share_ref[at, :] * thickness * slope_ref[at, :]
            col[o] = jnp.where(live_ref[at, :] > 0, value, -1.0)
        return carry

    lax.fori_loop(0, n_all // 4, chunk, 0)

    def move(frm, to, send, recv, peer, slot):
        return pltpu.make_async_remote_copy(
            src_ref=frm.at[peer], dst_ref=to.at[slot], send_sem=send.at[peer], recv_sem=recv.at[slot],
            device_id=where(peer), device_id_type=pl.DeviceIdType.MESH,
        )

    send3, recv3, send4, recv4 = sems[4:]
    others(n_all, me, lambda p: move(col, owned, send3, recv3, p, me).start())
    owned[pl.ds(me, 1)] = col[pl.ds(me, 1)]
    others(n_all, me, lambda p: move(col, owned, send3, recv3, p, p).wait_recv())
    column = owned[...]
    transmit = jnp.exp(-column)
    inverse = inv_ref[...]
    residual = jnp.where(column > -0.5, (obs_ref[...] - (1.0 - transmit)) * inverse, 0.0)
    res_ref[...] = residual
    pull[...] = jnp.where(column > -0.5, -residual * inverse * transmit, 0.0)
    others(n_all, me, lambda p: move(pull, back_ref, send4, recv4, p, me).start())
    back_ref[pl.ds(me, 1)] = pull[pl.ds(me, 1)]
    others(n_all, me, lambda p: move(pull, back_ref, send4, recv4, p, p).wait_recv())
    others(n_all, me, lambda p: move(col, owned, send3, recv3, p, me).wait_send())
    others(n_all, me, lambda p: move(pull, back_ref, send4, recv4, p, me).wait_send())

    def drain(t, carry):
        for copy in outward(t):
            copy.wait()
        pl.when(has_up)(lambda: upward(t).wait_send())
        pl.when(has_down)(lambda: downward(t).wait_send())
        return carry

    lax.fori_loop(0, tiles, drain, 0)


GROUP = 8
CHUNKS = 4


def scatter_kernel(
    n_own, row_ref, rows_ref, lo_ref, share_ref, pull_ref, mat_ref, pre_ref, off_ref,
    s_ref, tail_ref, ext_ref, imp_tab, near_tab, upd,
):
    step = pl.program_id(0)
    rows, width = s_ref.shape
    blocks = width // LANES
    first_phase = n_own // CHUNKS

    @pl.when(step == 0)
    def _():
        total = imp_tab.shape[0]

        def clear(i, carry):
            at = pl.ds(pl.multiple_of(i * 256, 256), 256)
            imp_tab[at, :] = jnp.zeros((256, LANES), jnp.float32)
            near_tab[at, :] = jnp.zeros((256, LANES), jnp.float32)
            return carry

        lax.fori_loop(0, total // 256, clear, 0)

    @pl.when(step < first_phase)
    def _():
        ext_ref[...] = pre_ref[...] + off_ref[...]
        sub = lax.broadcasted_iota(jnp.int32, (LANES, LANES), 0)
        lane = lax.broadcasted_iota(jnp.int32, (LANES, LANES), 1)
        grouped = sub // GROUP == lane // GROUP

        def chunk(o, carry):
            at = pl.ds(o, 1)
            same = jnp.broadcast_to(rows_ref[at, :], (LANES, LANES))
            same = jnp.logical_and(same == same.T, grouped)
            pull = pull_ref[o]
            a1, a2 = split2(jnp.where(same, pull, 0.0))
            b1, b2 = split2(jnp.where(same, pull * share_ref[at, :], 0.0))
            hot = (sub == lo_ref[at, :]).astype(jnp.bfloat16)
            out = lax.dot_general(
                jnp.concatenate([a1, a2, b1, b2], 0).astype(jnp.bfloat16),
                hot,
                (((1,), (1,)), ((), ())),
                preferred_element_type=jnp.float32,
            )
            upd[:LANES] = out[:LANES] + out[LANES : 2 * LANES]
            upd[LANES:] = out[2 * LANES : 3 * LANES] + out[3 * LANES :]
            for g in range(LANES // GROUP):
                cs = range(g * GROUP, (g + 1) * GROUP)
                where = [row_ref[o, c] for c in cs]
                imps = [imp_tab[pl.ds(w, 1), :] + upd[c : c + 1, :] for w, c in zip(where, cs)]
                nears = [near_tab[pl.ds(w, 1), :] + upd[LANES + c : LANES + c + 1, :] for w, c in zip(where, cs)]
                for w, a, b in zip(where, imps, nears):
                    imp_tab[pl.ds(w, 1), :] = a
                    near_tab[pl.ds(w, 1), :] = b
            return carry

        lax.fori_loop(step * CHUNKS, (step + 1) * CHUNKS, chunk, 0)

    def natural(tab):
        parts = []
        for b in range(blocks):
            at = pl.ds(pl.multiple_of(((step - first_phase) * blocks + b) * rows, rows), rows)
            parts.append(tab[at, :])
        return jnp.concatenate(parts, 1)

    @pl.when(step >= first_phase)
    def _():
        i1, i2 = split2(natural(imp_tab))
        n1, n2 = split2(natural(near_tab))
        out = jnp.dot(
            mat_ref[...],
            jnp.concatenate([i1, i2, n1, n2], 0).astype(jnp.bfloat16),
            preferred_element_type=jnp.float32,
        )
        s_ref[...] = out[:rows]
        tail_ref[...] = out[rows : rows + 1]


def body(excitation, star_shell, star_pixel, star_fraction, star_count, observed, inverse_error):
    rows, cols = excitation.shape
    size = lax.axis_size("shell")
    me = lax.axis_index("shell")
    thickness = depth_span / (rows * size)
    n_own = star_shell.shape[1]
    groups = cols // LANES
    tile = min(TILE, cols)
    f32, bf16 = jnp.float32, jnp.bfloat16

    pixel = star_pixel[0]
    hi, lo = pixel // LANES, pixel % LANES
    row = hi * rows + star_shell[0]
    share = 1.0 - star_fraction[0]
    live = (jnp.arange(LANES, dtype=jnp.int32)[None, :] < star_count[0][:, None]).astype(jnp.int32)

    mats = np.stack([stencil_matrix(rows, a, b) for a, b in ((0, 0), (1, 0), (0, 1), (1, 1))])
    top = mats.astype(bf16)
    rest = (mats - top.astype(np.float32)).astype(bf16)
    which = (me == 0).astype(jnp.int32) + 2 * (me == size - 1).astype(jnp.int32)
    mat = lax.dynamic_index_in_dim(jnp.asarray(np.concatenate([top, rest], 1)), which, 0, False)
    tri = np.tril(np.ones((rows, rows), np.float32))
    tri2 = jnp.asarray(np.concatenate([tri, tri], 1).astype(bf16))

    smem = pl.BlockSpec(memory_space=pltpu.SMEM)
    vmem = pl.BlockSpec(memory_space=pltpu.VMEM)
    full = lambda shape: pl.BlockSpec(shape, lambda i: (0, 0))
    stars = jax.ShapeDtypeStruct((n_own, LANES), f32)
    grid_shape = jax.ShapeDtypeStruct((rows, cols), f32)
    line = jax.ShapeDtypeStruct((1, cols), f32)
    limit = pltpu.CompilerParams(vmem_limit_bytes=48 * 2**20)

    n_sky = lax.axis_size("sky")
    n_all = size * n_sky
    spread = (size, groups // size, LANES)
    blocks = jax.ShapeDtypeStruct(spread, f32)
    slots = jax.ShapeDtypeStruct((n_all, 1, LANES), f32)
    hold = lambda like: pltpu.VMEM(like.shape, f32)
    dma = lambda k: pltpu.SemaphoreType.DMA((k,))

    def remote(number):
        return pltpu.CompilerParams(
            collective_id=number, has_side_effects=True, vmem_limit_bytes=48 * 2**20
        )

    tiles = cols // tile
    hbm = pl.BlockSpec(memory_space=pl.ANY)
    edge = pltpu.VMEM((tiles, PASSES, tile), f32)
    nat = pltpu.VMEM((tiles, rows, tile), f32)
    tab = pltpu.VMEM((groups * rows, LANES), f32)
    density, prefix, offset, residual, returned = pl.pallas_call(
        lambda *refs: field_kernel(size, n_sky, thickness, *refs),
        in_specs=[smem] + [vmem] * 9,
        out_specs=[hbm] * 2 + [vmem] * 3,
        out_shape=[grid_shape, grid_shape, blocks, slots, slots],
        scratch_shapes=[edge] * 4 + [nat] * 2 + [tab] * 2
        + [pltpu.VMEM((2, 2 * LANES, LANES), f32), hold(stars), hold(stars)]
        + [hold(blocks)] * 3 + [hold(slots)] * 3
        + [pltpu.SemaphoreType.DMA((2, tiles))] + [dma(tiles)] * 4 + [dma(size)] * 4 + [dma(n_all)] * 4,
        compiler_params=remote(0),
        name="field",
    )(row, excitation, mat, tri2, hi, lo, share, live, observed, inverse_error)

    upper = np.triu(np.ones((rows, rows), np.float32))
    eye = np.eye(rows, dtype=np.float32)
    top_row = np.zeros((16, 4 * rows), np.float32)
    top_row[0, : 2 * rows] = 1.0
    smat = jnp.asarray(
        np.concatenate([np.concatenate([upper, upper, -eye, -eye], 1), top_row], 0).astype(bf16)
    )
    early = n_own // CHUNKS
    ext_tile = cols // early
    out_tile = min(2 * TILE, cols)
    first = lambda r: pl.BlockSpec((r, ext_tile), lambda i: (0, jnp.minimum(i, early - 1)))
    second = lambda r: pl.BlockSpec((r, out_tile), lambda i: (0, jnp.maximum(i - early, 0)))
    local_sens, tails, extinction = pl.pallas_call(
        lambda *refs: scatter_kernel(n_own, *refs),
        grid=(early + cols // out_tile,),
        in_specs=[smem] + [full((n_own, LANES))] * 3
        + [pl.BlockSpec((n_own, 1, LANES), lambda i: (0, 0, 0)), full(smat.shape), first(rows), first(1)],
        out_specs=[second(rows), second(1), first(rows)],
        out_shape=[grid_shape, line, grid_shape],
        scratch_shapes=[
            pltpu.VMEM((groups * rows, LANES), f32),
            pltpu.VMEM((groups * rows, LANES), f32),
            pltpu.VMEM((2 * LANES, LANES), f32),
        ],
        compiler_params=limit,
        name="scatter",
    )(row, row.astype(f32), lo, share, returned, smat, prefix, offset.reshape(1, -1))

    tail_offset = pl.pallas_call(
        lambda *refs: tail_kernel(size, *refs),
        in_specs=[vmem],
        out_specs=vmem,
        out_shape=blocks,
        scratch_shapes=[hold(blocks), hold(blocks)] + [dma(size)] * 4,
        compiler_params=remote(1),
        name="tails",
    )(tails.reshape(spread))
    sensitivity = density * (local_sens + tail_offset.reshape(1, -1))
    return extinction, sensitivity, residual


def solution(mesh):
    stars = P(("shell", "sky"), None, None)
    owners = P(None, ("shell", "sky"), None)
    return jax.shard_map(
        body,
        mesh=mesh,
        in_specs=(P("shell", "sky"), stars, stars, stars, P(("shell", "sky"), None), owners, owners),
        out_specs=(P("shell", "sky"), P("shell", "sky"), owners),
        check_vma=False,
    )
```

```python
import jax
import jax.numpy as jnp
import numpy as np
from jax import lax
from jax.experimental import pallas as pl
from jax.experimental.pallas import tpu as pltpu
from jax.sharding import PartitionSpec as P

PASSES = 4
LANES = 128
TILE = 2048

depth_span = 2.0


def split2(x):
    high = x.astype(jnp.bfloat16).astype(jnp.float32)
    return high, x - high


def stencil_matrix(rows, first, last):
    wide = rows + 2 * PASSES
    valid = np.ones((wide, 1))
    if first:
        valid[:PASSES] = 0.0
    if last:
        valid[-PASSES:] = 0.0
    eye = np.eye(wide)
    out = eye
    for _ in range(PASSES):
        padded = np.pad(out, ((1, 1), (0, 0)))
        out = valid * (0.3 * (padded[:-2] + padded[2:]) + 0.35 * out + eye)
    out = out[PASSES:-PASSES]
    local = out[:, PASSES:-PASSES]
    halo = np.concatenate([out[:, :PASSES], out[:, -PASSES:]], 1)
    return np.concatenate([local, local, halo, halo], 1).astype(np.float32)


def others(count, me, act):
    def step(k, carry):
        act(lax.rem(me + k, count))
        return carry

    lax.fori_loop(1, count, step, 0)


def shell_exchange(n, me, upper, src, got, summed, out, sems, meanwhile=lambda half: None):
    send1, recv1, send2, recv2 = sems

    def move(frm, to, send, recv, peer, slot):
        return pltpu.make_async_remote_copy(
            src_ref=frm.at[peer], dst_ref=to.at[slot], send_sem=send.at[peer], recv_sem=recv.at[slot],
            device_id={"shell": peer}, device_id_type=pl.DeviceIdType.MESH,
        )

    others(n, me, lambda p: move(src, got, send1, recv1, p, me).start())
    got[pl.ds(me, 1)] = src[pl.ds(me, 1)]
    meanwhile(0)
    others(n, me, lambda p: move(src, got, send1, recv1, p, p).wait_recv())
    total = jnp.zeros(got.shape[1:], jnp.float32)
    for i in range(n):
        i = n - 1 - i if upper else i
        summed[i] = total
        total = total + got[i]
    others(n, me, lambda p: move(summed, out, send2, recv2, p, me).start())
    out[pl.ds(me, 1)] = summed[pl.ds(me, 1)]
    meanwhile(1)
    others(n, me, lambda p: move(summed, out, send2, recv2, p, p).wait_recv())
    others(n, me, lambda p: move(src, got, send1, recv1, p, me).wait_send())
    others(n, me, lambda p: move(summed, out, send2, recv2, p, me).wait_send())


def tail_kernel(n, src, out, got, summed, *sems):
    me = lax.axis_index("shell")
    barrier = pltpu.get_barrier_semaphore()
    others(n, me, lambda p: pl.semaphore_signal(
        barrier, inc=1, device_id={"shell": p}, device_id_type=pl.DeviceIdType.MESH))
    pl.semaphore_wait(barrier, n - 1)
    shell_exchange(n, me, True, src, got, summed, out, sems)


def field_kernel(
    n, n_sky, thickness, row_ref, count_ref, exc_ref, mat_ref, hi_ref, lo_ref, frac_ref, obs_hbm, inv_hbm,
    dens_out, pre_out, off_out, res_ref, back_ref,
    last4, first4, before, after, dens_nat, pre_nat, pre_tab, dens_tab, got_rows, base_ref, slope_ref,
    src, got, summed, col, owned, pull, obs_ref, inv_ref, in_sems, out_sems, up_send, up_recv, down_send, down_recv, *sems,
):
    shell = lax.axis_index("shell")
    me = shell * n_sky + lax.axis_index("sky")
    n_all = n * n_sky
    rows, cols = exc_ref.shape
    tiles, _, width = last4.shape
    blocks = width // LANES
    part = src.shape[1]
    where = lambda p: {"shell": p // n_sky, "sky": lax.rem(p, n_sky)}
    barrier = pltpu.get_barrier_semaphore()
    others(n_all, me, lambda p: pl.semaphore_signal(
        barrier, inc=1, device_id=where(p), device_id_type=pl.DeviceIdType.MESH))
    brought = [
        pltpu.make_async_copy(obs_hbm, obs_ref, in_sems.at[0]),
        pltpu.make_async_copy(inv_hbm, inv_ref, in_sems.at[1]),
    ]
    for copy in brought:
        copy.start()
    for t in range(tiles):
        at = slice(t * width, (t + 1) * width)
        last4[t] = exc_ref[rows - PASSES :, at]
        first4[t] = exc_ref[:PASSES, at]

    @pl.when(shell == 0)
    def _():
        before[...] = jnp.zeros(before.shape, jnp.float32)

    @pl.when(shell == n - 1)
    def _():
        after[...] = jnp.zeros(after.shape, jnp.float32)

    pl.semaphore_wait(barrier, n_all - 1)

    def upward(t):
        return pltpu.make_async_remote_copy(
            src_ref=last4.at[t], dst_ref=before.at[t], send_sem=up_send.at[t], recv_sem=up_recv.at[t],
            device_id={"shell": lax.rem(shell + 1, n)}, device_id_type=pl.DeviceIdType.MESH,
        )

    def downward(t):
        return pltpu.make_async_remote_copy(
            src_ref=first4.at[t], dst_ref=after.at[t], send_sem=down_send.at[t], recv_sem=down_recv.at[t],
            device_id={"shell": lax.rem(shell + n - 1, n)}, device_id_type=pl.DeviceIdType.MESH,
        )

    has_up, has_down = shell < n - 1, shell > 0

    def send(t, carry):
        pl.when(has_up)(lambda: upward(t).start())
        pl.when(has_down)(lambda: downward(t).start())
        return carry

    lax.fori_loop(0, tiles, send, 0)

    def outward(t):
        at = pl.ds(pl.multiple_of(t * width, width), width)
        return (
            pltpu.make_async_copy(dens_nat.at[t], dens_out.at[:, at], out_sems.at[0, t]),
            pltpu.make_async_copy(pre_nat.at[t], pre_out.at[:, at], out_sems.at[1, t]),
        )

    matrix = mat_ref[jnp.where(shell == 0, 1, 0) + jnp.where(shell == n - 1, 2, 0)]
    across = lax.broadcasted_iota(jnp.int32, (rows, 2 * rows), 1)
    across = jnp.where(across >= rows, across - rows, across)
    tri = (across <= lax.broadcasted_iota(jnp.int32, (rows, 2 * rows), 0)).astype(jnp.bfloat16)

    def tile(t, carry):
        pl.when(has_down)(lambda: upward(t).wait_recv())
        pl.when(has_up)(lambda: downward(t).wait_recv())
        e1, e2 = split2(exc_ref[:, pl.ds(pl.multiple_of(t * width, width), width)])
        h1, h2 = split2(jnp.concatenate([before[t], after[t]], 0))
        stacked = jnp.concatenate([e1, e2, h1, h2], 0).astype(jnp.bfloat16)
        both = jnp.dot(matrix, stacked, preferred_element_type=jnp.float32)
        dens = jnp.exp(both[:rows] + both[rows:])
        d1, d2 = split2(dens)
        pre = thickness * jnp.dot(
            tri,
            jnp.concatenate([d1, d2], 0).astype(jnp.bfloat16),
            preferred_element_type=jnp.float32,
        )
        dens_nat[t] = dens
        pre_nat[t] = pre
        for b in range(blocks):
            g = t * blocks + b
            at = pl.ds(pl.multiple_of(g * rows, rows), rows)
            pre_tab[at, :] = pre[:, b * LANES : (b + 1) * LANES]
            dens_tab[at, :] = dens[:, b * LANES : (b + 1) * LANES]
            src[g // part, pl.ds(lax.rem(g, part), 1), :] = pre[rows - 1 :, b * LANES : (b + 1) * LANES]
        for copy in outward(t):
            copy.start()
        return carry

    lax.fori_loop(0, tiles, tile, 0)
    lane = lax.broadcasted_iota(jnp.int32, (LANES, LANES), 1)
    sub = lax.broadcasted_iota(jnp.int32, (LANES, LANES), 0)

    def pick(quad, carry):
        for k in range(4):
            o = quad * 4 + k
            for c in range(LANES):
                at = row_ref[o, c]
                got_rows[k, c : c + 1, :] = pre_tab[pl.ds(at, 1), :]
                got_rows[k, LANES + c : LANES + c + 1, :] = dens_tab[pl.ds(at, 1), :]
        for k in range(4):
            o = quad * 4 + k
            hot = (sub == lo_ref[pl.ds(o, 1), :]).astype(jnp.bfloat16)
            g1, g2 = split2(got_rows[k])
            picked = jnp.dot(
                jnp.concatenate([g1, g2], 0).astype(jnp.bfloat16),
                hot,
                preferred_element_type=jnp.float32,
            )
            p = picked[:LANES] + picked[2 * LANES : 3 * LANES]
            d = picked[LANES : 2 * LANES] + picked[3 * LANES :]
            base_ref[pl.ds(o, 1), :] = jnp.sum(jnp.where(sub == lane, p, 0.0), 0, keepdims=True)
            slope_ref[pl.ds(o, 1), :] = jnp.sum(jnp.where(sub == lane, d, 0.0), 0, keepdims=True)
        return carry

    quads = n_all // 4
    cut = [0, quads // 2, quads]
    shell_exchange(
        n, shell, False, src, got, summed, off_out, sems[:4],
        lambda half: lax.fori_loop(cut[half], cut[half + 1], pick, 0),
    )

    groups = n * src.shape[1]
    o1, o2 = split2(off_out[...].reshape(groups, LANES))
    table = jnp.concatenate([o1.T, o2.T], 0).astype(jnp.bfloat16)
    tall = lax.broadcasted_iota(jnp.int32, (groups, LANES), 0)

    line = lax.broadcasted_iota(jnp.int32, (1, LANES), 1)

    def move(frm, to, send, recv, peer, slot):
        return pltpu.make_async_remote_copy(
            src_ref=frm.at[peer], dst_ref=to.at[slot], send_sem=send.at[peer], recv_sem=recv.at[slot],
            device_id=where(peer), device_id_type=pl.DeviceIdType.MESH,
        )

    send3, recv3, send4, recv4 = sems[4:]

    def push(p):
        pl.when(p != me)(lambda: move(col, owned, send3, recv3, p, me).start())

    def chunk(quad, carry):
        for k in range(4):
            o = quad * 4 + k
            at = pl.ds(o, 1)
            hot = (tall == hi_ref[at, :]).astype(jnp.bfloat16)
            off = jnp.dot(table, hot, preferred_element_type=jnp.float32)
            off = off[:LANES] + off[LANES:]
            off = jnp.sum(jnp.where(sub == lo_ref[at, :], off, 0.0), 0, keepdims=True)
            value = base_ref[at, :] + off - (1.0 - frac_ref[at, :]) * thickness * slope_ref[at, :]
            col[o] = jnp.where(line < count_ref[0, o], value, -1.0)
        for k in range(4):
            push(quad * 4 + k)
        return carry

    lax.fori_loop(0, n_all // 4, chunk, 0)

    owned[pl.ds(me, 1)] = col[pl.ds(me, 1)]
    others(n_all, me, lambda p: move(col, owned, send3, recv3, p, p).wait_recv())
    for copy in brought:
        copy.wait()
    column = owned[...]
    transmit = jnp.exp(-column)
    inverse = inv_ref[...]
    residual = jnp.where(column > -0.5, (obs_ref[...] - (1.0 - transmit)) * inverse, 0.0)
    res_ref[...] = residual
    pull[...] = jnp.where(column > -0.5, -residual * inverse * transmit, 0.0)
    others(n_all, me, lambda p: move(pull, back_ref, send4, recv4, p, me).start())
    back_ref[pl.ds(me, 1)] = pull[pl.ds(me, 1)]
    others(n_all, me, lambda p: move(pull, back_ref, send4, recv4, p, p).wait_recv())
    others(n_all, me, lambda p: move(col, owned, send3, recv3, p, me).wait_send())
    others(n_all, me, lambda p: move(pull, back_ref, send4, recv4, p, me).wait_send())

    def drain(t, carry):
        for copy in outward(t):
            copy.wait()
        pl.when(has_up)(lambda: upward(t).wait_send())
        pl.when(has_down)(lambda: downward(t).wait_send())
        return carry

    lax.fori_loop(0, tiles, drain, 0)


GROUP = 16
CHUNKS = 4


def scatter_kernel(
    n_own, row_ref, rows_ref, lo_ref, frac_ref, pull_ref, mat_ref, pre_ref, off_ref,
    s_ref, tail_ref, ext_ref, imp_tab, near_tab, upd,
):
    step = pl.program_id(0)
    rows, width = s_ref.shape
    blocks = width // LANES
    first_phase = n_own // CHUNKS

    @pl.when(step == 0)
    def _():
        total = imp_tab.shape[0]

        def clear(i, carry):
            at = pl.ds(pl.multiple_of(i * 256, 256), 256)
            imp_tab[at, :] = jnp.zeros((256, LANES), jnp.float32)
            near_tab[at, :] = jnp.zeros((256, LANES), jnp.float32)
            return carry

        lax.fori_loop(0, total // 256, clear, 0)

    @pl.when(step < first_phase)
    def _():
        ext_ref[...] = pre_ref[...] + off_ref[...]
        sub = lax.broadcasted_iota(jnp.int32, (LANES, LANES), 0)
        lane = lax.broadcasted_iota(jnp.int32, (LANES, LANES), 1)
        grouped = sub // GROUP == lane // GROUP

        for k in range(CHUNKS):
            o = step * CHUNKS + k
            at = pl.ds(o, 1)
            same = jnp.broadcast_to(rows_ref[at, :], (LANES, LANES))
            same = jnp.logical_and(same == same.T, grouped)
            pull = pull_ref[o]
            a1, a2 = split2(jnp.where(same, pull, 0.0))
            b1, b2 = split2(jnp.where(same, pull * (1.0 - frac_ref[at, :]), 0.0))
            hot = (sub == lo_ref[at, :]).astype(jnp.bfloat16)
            out = lax.dot_general(
                jnp.concatenate([a1, a2, b1, b2], 0).astype(jnp.bfloat16),
                hot,
                (((1,), (1,)), ((), ())),
                preferred_element_type=jnp.float32,
            )
            upd[k, :LANES] = out[:LANES] + out[LANES : 2 * LANES]
            upd[k, LANES:] = out[2 * LANES : 3 * LANES] + out[3 * LANES :]
        for k in range(CHUNKS):
            o = step * CHUNKS + k
            for g in range(LANES // GROUP):
                cs = range(g * GROUP, (g + 1) * GROUP)
                where = [row_ref[o, c] for c in cs]
                imps = [imp_tab[pl.ds(w, 1), :] + upd[k, c : c + 1, :] for w, c in zip(where, cs)]
                nears = [near_tab[pl.ds(w, 1), :] + upd[k, LANES + c : LANES + c + 1, :] for w, c in zip(where, cs)]
                for w, a, b in zip(where, imps, nears):
                    imp_tab[pl.ds(w, 1), :] = a
                    near_tab[pl.ds(w, 1), :] = b

    def natural(tab):
        parts = []
        for b in range(blocks):
            at = pl.ds(pl.multiple_of(((step - first_phase) * blocks + b) * rows, rows), rows)
            parts.append(tab[at, :])
        return jnp.concatenate(parts, 1)

    @pl.when(step >= first_phase)
    def _():
        i1, i2 = split2(natural(imp_tab))
        n1, n2 = split2(natural(near_tab))
        out = jnp.dot(
            mat_ref[...],
            jnp.concatenate([i1, i2, n1, n2], 0).astype(jnp.bfloat16),
            preferred_element_type=jnp.float32,
        )
        s_ref[...] = out[:rows]
        tail_ref[...] = out[rows : rows + 1]


def body(excitation, star_shell, star_pixel, star_fraction, star_count, observed, inverse_error):
    rows, cols = excitation.shape
    size = lax.axis_size("shell")
    thickness = depth_span / (rows * size)
    n_own = star_shell.shape[1]
    groups = cols // LANES
    tile = min(TILE, cols)
    f32, bf16 = jnp.float32, jnp.bfloat16

    pixel = star_pixel[0]
    hi, lo = pixel // LANES, pixel % LANES
    row = hi * rows + star_shell[0]
    mats = np.stack([stencil_matrix(rows, a, b) for a, b in ((0, 0), (1, 0), (0, 1), (1, 1))])
    top = mats.astype(bf16)
    rest = (mats - top.astype(np.float32)).astype(bf16)
    mat = jnp.asarray(np.concatenate([top, rest], 1))

    smem = pl.BlockSpec(memory_space=pltpu.SMEM)
    vmem = pl.BlockSpec(memory_space=pltpu.VMEM)
    full = lambda shape: pl.BlockSpec(shape, lambda i: (0, 0))
    stars = jax.ShapeDtypeStruct((n_own, LANES), f32)
    grid_shape = jax.ShapeDtypeStruct((rows, cols), f32)
    line = jax.ShapeDtypeStruct((1, cols), f32)
    limit = pltpu.CompilerParams(vmem_limit_bytes=48 * 2**20)

    n_sky = lax.axis_size("sky")
    n_all = size * n_sky
    spread = (size, groups // size, LANES)
    blocks = jax.ShapeDtypeStruct(spread, f32)
    slots = jax.ShapeDtypeStruct((n_all, 1, LANES), f32)
    hold = lambda like: pltpu.VMEM(like.shape, f32)
    dma = lambda k: pltpu.SemaphoreType.DMA((k,))

    def remote(number):
        return pltpu.CompilerParams(
            collective_id=number, has_side_effects=True, vmem_limit_bytes=48 * 2**20
        )

    tiles = cols // tile
    hbm = pl.BlockSpec(memory_space=pl.ANY)
    edge = pltpu.VMEM((tiles, PASSES, tile), f32)
    nat = pltpu.VMEM((tiles, rows, tile), f32)
    tab = pltpu.VMEM((groups * rows, LANES), f32)
    density, prefix, offset, residual, returned = pl.pallas_call(
        lambda *refs: field_kernel(size, n_sky, thickness, *refs),
        in_specs=[smem] * 2 + [vmem] * 5 + [hbm] * 2,
        out_specs=[hbm] * 2 + [vmem] * 3,
        out_shape=[grid_shape, grid_shape, blocks, slots, slots],
        scratch_shapes=[edge] * 4 + [nat] * 2 + [tab] * 2
        + [pltpu.VMEM((4, 2 * LANES, LANES), f32), hold(stars), hold(stars)]
        + [hold(blocks)] * 3 + [hold(slots)] * 5
        + [dma(2), pltpu.SemaphoreType.DMA((2, tiles))] + [dma(tiles)] * 4 + [dma(size)] * 4 + [dma(n_all)] * 4,
        compiler_params=remote(0),
        name="field",
    )(row, star_count, excitation, mat, hi, lo, star_fraction[0], observed, inverse_error)

    upper = np.triu(np.ones((rows, rows), np.float32))
    eye = np.eye(rows, dtype=np.float32)
    top_row = np.zeros((16, 4 * rows), np.float32)
    top_row[0, : 2 * rows] = 1.0
    smat = jnp.asarray(
        np.concatenate([np.concatenate([upper, upper, -eye, -eye], 1), top_row], 0).astype(bf16)
    )
    early = n_own // CHUNKS
    ext_tile = cols // early
    out_tile = min(2 * TILE, cols)
    first = lambda r: pl.BlockSpec((r, ext_tile), lambda i: (0, jnp.minimum(i, early - 1)))
    second = lambda r: pl.BlockSpec((r, out_tile), lambda i: (0, jnp.maximum(i - early, 0)))
    local_sens, tails, extinction = pl.pallas_call(
        lambda *refs: scatter_kernel(n_own, *refs),
        grid=(early + cols // out_tile,),
        in_specs=[smem] + [full((n_own, LANES))] * 3
        + [pl.BlockSpec((n_own, 1, LANES), lambda i: (0, 0, 0)), full(smat.shape), first(rows), first(1)],
        out_specs=[second(rows), second(1), first(rows)],
        out_shape=[grid_shape, line, grid_shape],
        scratch_shapes=[
            pltpu.VMEM((groups * rows, LANES), f32),
            pltpu.VMEM((groups * rows, LANES), f32),
            pltpu.VMEM((CHUNKS, 2 * LANES, LANES), f32),
        ],
        compiler_params=limit,
        name="scatter",
    )(row, row.astype(f32), lo, star_fraction[0], returned, smat, prefix, offset.reshape(1, -1))

    tail_offset = pl.pallas_call(
        lambda *refs: tail_kernel(size, *refs),
        in_specs=[vmem],
        out_specs=vmem,
        out_shape=blocks,
        scratch_shapes=[hold(blocks), hold(blocks)] + [dma(size)] * 4,
        compiler_params=remote(1),
        name="tails",
    )(tails.reshape(spread))
    sensitivity = density * (local_sens + tail_offset.reshape(1, -1))
    return extinction, sensitivity, residual


def solution(mesh):
    stars = P(("shell", "sky"), None, None)
    owners = P(None, ("shell", "sky"), None)
    return jax.shard_map(
        body,
        mesh=mesh,
        in_specs=(P("shell", "sky"), stars, stars, stars, P(("shell", "sky"), None), owners, owners),
        out_specs=(P("shell", "sky"), P("shell", "sky"), owners),
        check_vma=False,
    )
```

```python
import jax
import jax.numpy as jnp
import numpy as np
from jax import lax
from jax.experimental import pallas as pl
from jax.experimental.pallas import tpu as pltpu
from jax.sharding import PartitionSpec as P

PASSES = 4
LANES = 128
TILE = 2048

depth_span = 2.0


def split2(x):
    high = x.astype(jnp.bfloat16).astype(jnp.float32)
    return high, x - high


def stencil_matrix(rows, first, last):
    pad = 2 * PASSES
    shape = (rows + 2 * pad, 2 * rows + 4 * PASSES)
    at = lax.broadcasted_iota(jnp.int32, shape, 0)
    col = lax.broadcasted_iota(jnp.int32, shape, 1)
    local = jnp.where(col >= rows, col - rows, col) + pad
    halo = col - 2 * rows
    halo = jnp.where(halo >= 2 * PASSES, halo - 2 * PASSES, halo)
    halo = jnp.where(halo < PASSES, halo + PASSES, halo + rows + PASSES)
    eye = jnp.where(at == jnp.where(col < 2 * rows, local, halo), 1.0, 0.0)
    low = jnp.where(first, pad, 0)
    high = jnp.where(last, rows + pad, rows + 2 * pad)
    valid = jnp.where(jnp.logical_and(at >= low, at < high), 1.0, 0.0)
    edge = jnp.zeros((1, shape[1]), jnp.float32)
    out = eye
    for _ in range(PASSES):
        beside = jnp.concatenate([edge, out[:-1]], 0) + jnp.concatenate([out[1:], edge], 0)
        out = valid * (0.3 * beside + 0.35 * out + eye)
    top, rest = split2(out[pad:-pad])
    return jnp.concatenate([top, rest], 0).astype(jnp.bfloat16)


def others(count, me, act):
    def step(k, carry):
        act(lax.rem(me + k, count))
        return carry

    lax.fori_loop(1, count, step, 0)


def shell_exchange(n, me, upper, src, got, summed, out, sems, meanwhile=lambda half: None):
    send1, recv1, send2, recv2 = sems

    def move(frm, to, send, recv, peer, slot):
        return pltpu.make_async_remote_copy(
            src_ref=frm.at[peer], dst_ref=to.at[slot], send_sem=send.at[peer], recv_sem=recv.at[slot],
            device_id={"shell": peer}, device_id_type=pl.DeviceIdType.MESH,
        )

    others(n, me, lambda p: move(src, got, send1, recv1, p, me).start())
    got[pl.ds(me, 1)] = src[pl.ds(me, 1)]
    meanwhile(0)
    others(n, me, lambda p: move(src, got, send1, recv1, p, p).wait_recv())
    total = jnp.zeros(got.shape[1:], jnp.float32)
    for i in range(n):
        i = n - 1 - i if upper else i
        summed[i] = total
        total = total + got[i]
    others(n, me, lambda p: move(summed, out, send2, recv2, p, me).start())
    out[pl.ds(me, 1)] = summed[pl.ds(me, 1)]
    meanwhile(1)
    others(n, me, lambda p: move(summed, out, send2, recv2, p, p).wait_recv())
    others(n, me, lambda p: move(src, got, send1, recv1, p, me).wait_send())
    others(n, me, lambda p: move(summed, out, send2, recv2, p, me).wait_send())


def tail_kernel(n, src, out, got, summed, *sems):
    me = lax.axis_index("shell")
    barrier = pltpu.get_barrier_semaphore()
    others(n, me, lambda p: pl.semaphore_signal(
        barrier, inc=1, device_id={"shell": p}, device_id_type=pl.DeviceIdType.MESH))
    pl.semaphore_wait(barrier, n - 1)
    shell_exchange(n, me, True, src, got, summed, out, sems)


def field_kernel(
    n, n_sky, thickness, row_ref, hi_ref, lo_ref, exc_hbm, frac_hbm, obs_hbm, inv_hbm,
    dens_out, pre_out, off_out, res_ref, back_ref,
    last4, first4, before, after, dens_nat, pre_nat, pre_tab, dens_tab, got_rows, base_ref, slope_ref,
    src, got, summed, col, owned, pull, exc_ref, frac_ref, obs_ref, inv_ref, in_sems, out_sems, up_send, up_recv, down_send, down_recv, *sems,
):
    shell = lax.axis_index("shell")
    me = shell * n_sky + lax.axis_index("sky")
    n_all = n * n_sky
    pairs = (
        (exc_hbm, exc_ref), (frac_hbm, frac_ref), (obs_hbm, obs_ref), (inv_hbm, inv_ref),
    )
    brought = [pltpu.make_async_copy(a, b, in_sems.at[i]) for i, (a, b) in enumerate(pairs)]
    for copy in brought:
        copy.start()
    rows, cols = exc_ref.shape
    tiles, _, width = last4.shape
    blocks = width // LANES
    part = src.shape[1]
    where = lambda p: {"shell": p // n_sky, "sky": lax.rem(p, n_sky)}
    barrier = pltpu.get_barrier_semaphore()
    others(n_all, me, lambda p: pl.semaphore_signal(
        barrier, inc=1, device_id=where(p), device_id_type=pl.DeviceIdType.MESH))
    matrix = stencil_matrix(rows, shell == 0, shell == n - 1)
    brought[0].wait()
    for t in range(tiles):
        at = slice(t * width, (t + 1) * width)
        last4[t] = exc_ref[rows - PASSES :, at]
        first4[t] = exc_ref[:PASSES, at]

    @pl.when(shell == 0)
    def _():
        before[...] = jnp.zeros(before.shape, jnp.float32)

    @pl.when(shell == n - 1)
    def _():
        after[...] = jnp.zeros(after.shape, jnp.float32)

    pl.semaphore_wait(barrier, n_all - 1)

    def upward(t):
        return pltpu.make_async_remote_copy(
            src_ref=last4.at[t], dst_ref=before.at[t], send_sem=up_send.at[t], recv_sem=up_recv.at[t],
            device_id={"shell": lax.rem(shell + 1, n)}, device_id_type=pl.DeviceIdType.MESH,
        )

    def downward(t):
        return pltpu.make_async_remote_copy(
            src_ref=first4.at[t], dst_ref=after.at[t], send_sem=down_send.at[t], recv_sem=down_recv.at[t],
            device_id={"shell": lax.rem(shell + n - 1, n)}, device_id_type=pl.DeviceIdType.MESH,
        )

    has_up, has_down = shell < n - 1, shell > 0

    def send(t, carry):
        pl.when(has_up)(lambda: upward(t).start())
        pl.when(has_down)(lambda: downward(t).start())
        return carry

    lax.fori_loop(0, tiles, send, 0)

    def outward(t):
        at = pl.ds(pl.multiple_of(t * width, width), width)
        return (
            pltpu.make_async_copy(dens_nat.at[t], dens_out.at[:, at], out_sems.at[0, t]),
            pltpu.make_async_copy(pre_nat.at[t], pre_out.at[:, at], out_sems.at[1, t]),
        )

    for copy in brought[1:]:
        copy.wait()
    across = lax.broadcasted_iota(jnp.int32, (rows, 2 * rows), 1)
    across = jnp.where(across >= rows, across - rows, across)
    tri = (across <= lax.broadcasted_iota(jnp.int32, (rows, 2 * rows), 0)).astype(jnp.bfloat16)

    def tile(t, carry):
        pl.when(has_down)(lambda: upward(t).wait_recv())
        pl.when(has_up)(lambda: downward(t).wait_recv())
        e1, e2 = split2(exc_ref[:, pl.ds(pl.multiple_of(t * width, width), width)])
        h1, h2 = split2(jnp.concatenate([before[t], after[t]], 0))
        stacked = jnp.concatenate([e1, e2, h1, h2], 0).astype(jnp.bfloat16)
        both = jnp.dot(matrix, stacked, preferred_element_type=jnp.float32)
        dens = jnp.exp(both[:rows] + both[rows:])
        d1, d2 = split2(dens)
        pre = thickness * jnp.dot(
            tri,
            jnp.concatenate([d1, d2], 0).astype(jnp.bfloat16),
            preferred_element_type=jnp.float32,
        )
        dens_nat[t] = dens
        pre_nat[t] = pre
        for b in range(blocks):
            g = t * blocks + b
            at = pl.ds(pl.multiple_of(g * rows, rows), rows)
            pre_tab[at, :] = pre[:, b * LANES : (b + 1) * LANES]
            dens_tab[at, :] = dens[:, b * LANES : (b + 1) * LANES]
            src[g // part, pl.ds(lax.rem(g, part), 1), :] = pre[rows - 1 :, b * LANES : (b + 1) * LANES]
        for copy in outward(t):
            copy.start()
        return carry

    lax.fori_loop(0, tiles, tile, 0)
    lane = lax.broadcasted_iota(jnp.int32, (LANES, LANES), 1)
    sub = lax.broadcasted_iota(jnp.int32, (LANES, LANES), 0)

    def pick(quad, carry):
        for k in range(4):
            o = quad * 4 + k
            for c in range(LANES):
                at = row_ref[o, c]
                got_rows[k, c : c + 1, :] = pre_tab[pl.ds(at, 1), :]
                got_rows[k, LANES + c : LANES + c + 1, :] = dens_tab[pl.ds(at, 1), :]
        for k in range(4):
            o = quad * 4 + k
            hot = (sub == lo_ref[pl.ds(o, 1), :]).astype(jnp.bfloat16)
            g1, g2 = split2(got_rows[k])
            picked = jnp.dot(
                jnp.concatenate([g1, g2], 0).astype(jnp.bfloat16),
                hot,
                preferred_element_type=jnp.float32,
            )
            p = picked[:LANES] + picked[2 * LANES : 3 * LANES]
            d = picked[LANES : 2 * LANES] + picked[3 * LANES :]
            base_ref[pl.ds(o, 1), :] = jnp.sum(jnp.where(sub == lane, p, 0.0), 0, keepdims=True)
            slope_ref[pl.ds(o, 1), :] = jnp.sum(jnp.where(sub == lane, d, 0.0), 0, keepdims=True)
        return carry

    quads = n_all // 4
    cut = [0, quads // 2, quads]
    shell_exchange(
        n, shell, False, src, got, summed, off_out, sems[:4],
        lambda half: lax.fori_loop(cut[half], cut[half + 1], pick, 0),
    )

    groups = n * src.shape[1]
    o1, o2 = split2(off_out[...].reshape(groups, LANES))
    table = jnp.concatenate([o1.T, o2.T], 0).astype(jnp.bfloat16)
    tall = lax.broadcasted_iota(jnp.int32, (groups, LANES), 0)

    def move(frm, to, send, recv, peer, slot):
        return pltpu.make_async_remote_copy(
            src_ref=frm.at[peer], dst_ref=to.at[slot], send_sem=send.at[peer], recv_sem=recv.at[slot],
            device_id=where(peer), device_id_type=pl.DeviceIdType.MESH,
        )

    send3, recv3, send4, recv4 = sems[4:]

    def push(p):
        pl.when(p != me)(lambda: move(col, owned, send3, recv3, p, me).start())

    def chunk(quad, carry):
        for k in range(4):
            o = quad * 4 + k
            at = pl.ds(o, 1)
            hot = (tall == hi_ref[at, :]).astype(jnp.bfloat16)
            off = jnp.dot(table, hot, preferred_element_type=jnp.float32)
            off = off[:LANES] + off[LANES:]
            off = jnp.sum(jnp.where(sub == lo_ref[at, :], off, 0.0), 0, keepdims=True)
            value = base_ref[at, :] + off - (1.0 - frac_ref[at, :]) * thickness * slope_ref[at, :]
            col[o] = jnp.where(hi_ref[at, :] < groups, value, -1.0)
        for k in range(4):
            push(quad * 4 + k)
        return carry

    lax.fori_loop(0, n_all // 4, chunk, 0)

    owned[pl.ds(me, 1)] = col[pl.ds(me, 1)]
    others(n_all, me, lambda p: move(col, owned, send3, recv3, p, p).wait_recv())
    column = owned[...]
    transmit = jnp.exp(-column)
    inverse = inv_ref[...]
    residual = jnp.where(column > -0.5, (obs_ref[...] - (1.0 - transmit)) * inverse, 0.0)
    res_ref[...] = residual
    pull[...] = jnp.where(column > -0.5, -residual * inverse * transmit, 0.0)
    others(n_all, me, lambda p: move(pull, back_ref, send4, recv4, p, me).start())
    back_ref[pl.ds(me, 1)] = pull[pl.ds(me, 1)]
    others(n_all, me, lambda p: move(pull, back_ref, send4, recv4, p, p).wait_recv())
    others(n_all, me, lambda p: move(col, owned, send3, recv3, p, me).wait_send())
    others(n_all, me, lambda p: move(pull, back_ref, send4, recv4, p, me).wait_send())

    def drain(t, carry):
        for copy in outward(t):
            copy.wait()
        pl.when(has_up)(lambda: upward(t).wait_send())
        pl.when(has_down)(lambda: downward(t).wait_send())
        return carry

    lax.fori_loop(0, tiles, drain, 0)


GROUP = 16
CHUNKS = 4


def scatter_kernel(
    n_own, row_ref, rows_ref, lo_ref, frac_ref, pull_ref, mat_ref, pre_ref, off_ref,
    s_ref, tail_ref, ext_ref, imp_tab, near_tab, upd,
):
    step = pl.program_id(0)
    rows, width = s_ref.shape
    blocks = width // LANES
    first_phase = n_own // CHUNKS

    @pl.when(step == 0)
    def _():
        total = imp_tab.shape[0]

        def clear(i, carry):
            at = pl.ds(pl.multiple_of(i * 256, 256), 256)
            imp_tab[at, :] = jnp.zeros((256, LANES), jnp.float32)
            near_tab[at, :] = jnp.zeros((256, LANES), jnp.float32)
            return carry

        lax.fori_loop(0, total // 256, clear, 0)

    @pl.when(step < first_phase)
    def _():
        ext_ref[...] = pre_ref[...] + off_ref[...]
        sub = lax.broadcasted_iota(jnp.int32, (LANES, LANES), 0)
        lane = lax.broadcasted_iota(jnp.int32, (LANES, LANES), 1)
        grouped = sub // GROUP == lane // GROUP

        for k in range(CHUNKS):
            o = step * CHUNKS + k
            at = pl.ds(o, 1)
            same = jnp.broadcast_to(rows_ref[at, :], (LANES, LANES))
            same = jnp.logical_and(same == same.T, grouped)
            pull = pull_ref[o]
            a1, a2 = split2(jnp.where(same, pull, 0.0))
            b1, b2 = split2(jnp.where(same, pull * (1.0 - frac_ref[at, :]), 0.0))
            hot = (sub == lo_ref[at, :]).astype(jnp.bfloat16)
            out = lax.dot_general(
                jnp.concatenate([a1, a2, b1, b2], 0).astype(jnp.bfloat16),
                hot,
                (((1,), (1,)), ((), ())),
                preferred_element_type=jnp.float32,
            )
            upd[k, :LANES] = out[:LANES] + out[LANES : 2 * LANES]
            upd[k, LANES:] = out[2 * LANES : 3 * LANES] + out[3 * LANES :]
        for k in range(CHUNKS):
            o = step * CHUNKS + k
            for g in range(LANES // GROUP):
                cs = range(g * GROUP, (g + 1) * GROUP)
                where = [row_ref[o, c] for c in cs]
                imps = [imp_tab[pl.ds(w, 1), :] + upd[k, c : c + 1, :] for w, c in zip(where, cs)]
                nears = [near_tab[pl.ds(w, 1), :] + upd[k, LANES + c : LANES + c + 1, :] for w, c in zip(where, cs)]
                for w, a, b in zip(where, imps, nears):
                    imp_tab[pl.ds(w, 1), :] = a
                    near_tab[pl.ds(w, 1), :] = b

    def natural(tab):
        parts = []
        for b in range(blocks):
            at = pl.ds(pl.multiple_of(((step - first_phase) * blocks + b) * rows, rows), rows)
            parts.append(tab[at, :])
        return jnp.concatenate(parts, 1)

    @pl.when(step >= first_phase)
    def _():
        i1, i2 = split2(natural(imp_tab))
        n1, n2 = split2(natural(near_tab))
        out = jnp.dot(
            mat_ref[...],
            jnp.concatenate([i1, i2, n1, n2], 0).astype(jnp.bfloat16),
            preferred_element_type=jnp.float32,
        )
        s_ref[...] = out[:rows]
        tail_ref[...] = out[rows : rows + 1]


def body(excitation, star_shell, star_pixel, star_fraction, star_count, observed, inverse_error):
    rows, cols = excitation.shape
    size = lax.axis_size("shell")
    thickness = depth_span / (rows * size)
    n_own = star_shell.shape[1]
    groups = cols // LANES
    tile = min(TILE, cols)
    f32, bf16 = jnp.float32, jnp.bfloat16

    pixel = star_pixel[0]
    hi, lo = pixel // LANES, pixel % LANES
    row = hi * rows + star_shell[0]
    live = jnp.arange(LANES, dtype=jnp.int32)[None, :] < star_count[0][:, None]
    hi = jnp.where(live, hi, groups)

    smem = pl.BlockSpec(memory_space=pltpu.SMEM)
    vmem = pl.BlockSpec(memory_space=pltpu.VMEM)
    full = lambda shape: pl.BlockSpec(shape, lambda i: (0, 0))
    stars = jax.ShapeDtypeStruct((n_own, LANES), f32)
    grid_shape = jax.ShapeDtypeStruct((rows, cols), f32)
    line = jax.ShapeDtypeStruct((1, cols), f32)
    limit = pltpu.CompilerParams(vmem_limit_bytes=48 * 2**20)

    n_sky = lax.axis_size("sky")
    n_all = size * n_sky
    spread = (size, groups // size, LANES)
    blocks = jax.ShapeDtypeStruct(spread, f32)
    slots = jax.ShapeDtypeStruct((n_all, 1, LANES), f32)
    hold = lambda like: pltpu.VMEM(like.shape, f32)
    dma = lambda k: pltpu.SemaphoreType.DMA((k,))

    def remote(number):
        return pltpu.CompilerParams(
            collective_id=number, has_side_effects=True, vmem_limit_bytes=48 * 2**20
        )

    tiles = cols // tile
    hbm = pl.BlockSpec(memory_space=pl.ANY)
    edge = pltpu.VMEM((tiles, PASSES, tile), f32)
    nat = pltpu.VMEM((tiles, rows, tile), f32)
    tab = pltpu.VMEM((groups * rows, LANES), f32)
    density, prefix, offset, residual, returned = pl.pallas_call(
        lambda *refs: field_kernel(size, n_sky, thickness, *refs),
        in_specs=[smem, vmem, vmem] + [hbm] * 4,
        out_specs=[hbm] * 2 + [vmem] * 3,
        out_shape=[grid_shape, grid_shape, blocks, slots, slots],
        scratch_shapes=[edge] * 4 + [nat] * 2 + [tab] * 2
        + [pltpu.VMEM((4, 2 * LANES, LANES), f32), hold(stars), hold(stars)]
        + [hold(blocks)] * 3 + [hold(slots)] * 3
        + [pltpu.VMEM((rows, cols), f32), hold(stars), hold(slots), hold(slots)]
        + [dma(4), pltpu.SemaphoreType.DMA((2, tiles))] + [dma(tiles)] * 4 + [dma(size)] * 4 + [dma(n_all)] * 4,
        compiler_params=remote(0),
        name="field",
    )(row, hi, lo, excitation, star_fraction[0], observed, inverse_error)

    upper = np.triu(np.ones((rows, rows), np.float32))
    eye = np.eye(rows, dtype=np.float32)
    top_row = np.zeros((16, 4 * rows), np.float32)
    top_row[0, : 2 * rows] = 1.0
    smat = jnp.asarray(
        np.concatenate([np.concatenate([upper, upper, -eye, -eye], 1), top_row], 0).astype(bf16)
    )
    early = n_own // CHUNKS
    ext_tile = cols // early
    out_tile = min(2 * TILE, cols)
    first = lambda r: pl.BlockSpec((r, ext_tile), lambda i: (0, jnp.minimum(i, early - 1)))
    second = lambda r: pl.BlockSpec((r, out_tile), lambda i: (0, jnp.maximum(i - early, 0)))
    local_sens, tails, extinction = pl.pallas_call(
        lambda *refs: scatter_kernel(n_own, *refs),
        grid=(early + cols // out_tile,),
        in_specs=[smem] + [full((n_own, LANES))] * 3
        + [pl.BlockSpec((n_own, 1, LANES), lambda i: (0, 0, 0)), full(smat.shape), first(rows), first(1)],
        out_specs=[second(rows), second(1), first(rows)],
        out_shape=[grid_shape, line, grid_shape],
        scratch_shapes=[
            pltpu.VMEM((groups * rows, LANES), f32),
            pltpu.VMEM((groups * rows, LANES), f32),
            pltpu.VMEM((CHUNKS, 2 * LANES, LANES), f32),
        ],
        compiler_params=limit,
        name="scatter",
    )(row, row.astype(f32), lo, star_fraction[0], returned, smat, prefix, offset.reshape(1, -1))

    tail_offset = pl.pallas_call(
        lambda *refs: tail_kernel(size, *refs),
        in_specs=[vmem],
        out_specs=vmem,
        out_shape=blocks,
        scratch_shapes=[hold(blocks), hold(blocks)] + [dma(size)] * 4,
        compiler_params=remote(1),
        name="tails",
    )(tails.reshape(spread))
    sensitivity = density * (local_sens + tail_offset.reshape(1, -1))
    return extinction, sensitivity, residual


def solution(mesh):
    stars = P(("shell", "sky"), None, None)
    owners = P(None, ("shell", "sky"), None)
    return jax.shard_map(
        body,
        mesh=mesh,
        in_specs=(P("shell", "sky"), stars, stars, stars, P(("shell", "sky"), None), owners, owners),
        out_specs=(P("shell", "sky"), P("shell", "sky"), owners),
        check_vma=False,
    )
```

```python
import jax
import jax.numpy as jnp
import numpy as np
from jax import lax
from jax.experimental import pallas as pl
from jax.experimental.pallas import tpu as pltpu
from jax.sharding import PartitionSpec as P

PASSES = 4
LANES = 128
TILE = 2048

depth_span = 2.0


def split2(x):
    high = x.astype(jnp.bfloat16).astype(jnp.float32)
    return high, x - high


def stencil_matrix(rows, first, last):
    pad = 2 * PASSES
    shape = (rows + 2 * pad, 2 * rows + 4 * PASSES)
    at = lax.broadcasted_iota(jnp.int32, shape, 0)
    col = lax.broadcasted_iota(jnp.int32, shape, 1)
    local = jnp.where(col >= rows, col - rows, col) + pad
    halo = col - 2 * rows
    halo = jnp.where(halo >= 2 * PASSES, halo - 2 * PASSES, halo)
    halo = jnp.where(halo < PASSES, halo + PASSES, halo + rows + PASSES)
    eye = jnp.where(at == jnp.where(col < 2 * rows, local, halo), 1.0, 0.0)
    low = jnp.where(first, pad, 0)
    high = jnp.where(last, rows + pad, rows + 2 * pad)
    valid = jnp.where(jnp.logical_and(at >= low, at < high), 1.0, 0.0)
    edge = jnp.zeros((1, shape[1]), jnp.float32)
    out = eye
    for _ in range(PASSES):
        beside = jnp.concatenate([edge, out[:-1]], 0) + jnp.concatenate([out[1:], edge], 0)
        out = valid * (0.3 * beside + 0.35 * out + eye)
    top, rest = split2(out[pad:-pad])
    return jnp.concatenate([top, rest], 0).astype(jnp.bfloat16)


def others(count, me, act):
    def step(k, carry):
        act(lax.rem(me + k, count))
        return carry

    lax.fori_loop(1, count, step, 0)


def shell_exchange(n, me, upper, src, got, summed, out, sems, meanwhile=lambda half: None):
    send1, recv1, send2, recv2 = sems

    def move(frm, to, send, recv, peer, slot):
        return pltpu.make_async_remote_copy(
            src_ref=frm.at[peer], dst_ref=to.at[slot], send_sem=send.at[peer], recv_sem=recv.at[slot],
            device_id={"shell": peer}, device_id_type=pl.DeviceIdType.MESH,
        )

    others(n, me, lambda p: move(src, got, send1, recv1, p, me).start())
    got[pl.ds(me, 1)] = src[pl.ds(me, 1)]
    meanwhile(0)
    others(n, me, lambda p: move(src, got, send1, recv1, p, p).wait_recv())
    total = jnp.zeros(got.shape[1:], jnp.float32)
    for i in range(n):
        i = n - 1 - i if upper else i
        summed[i] = total
        total = total + got[i]
    others(n, me, lambda p: move(summed, out, send2, recv2, p, me).start())
    out[pl.ds(me, 1)] = summed[pl.ds(me, 1)]
    meanwhile(1)
    others(n, me, lambda p: move(summed, out, send2, recv2, p, p).wait_recv())
    others(n, me, lambda p: move(src, got, send1, recv1, p, me).wait_send())
    others(n, me, lambda p: move(summed, out, send2, recv2, p, me).wait_send())


def tail_kernel(n, src, out, got, summed, *sems):
    me = lax.axis_index("shell")
    barrier = pltpu.get_barrier_semaphore()
    others(n, me, lambda p: pl.semaphore_signal(
        barrier, inc=1, device_id={"shell": p}, device_id_type=pl.DeviceIdType.MESH))
    pl.semaphore_wait(barrier, n - 1)
    shell_exchange(n, me, True, src, got, summed, out, sems)


def field_kernel(
    n, n_sky, thickness, row_ref, hi_ref, lo_ref, exc_hbm, frac_hbm, obs_hbm, inv_hbm,
    dens_out, pre_out, off_out, res_ref, back_ref,
    last4, first4, before, after, dens_nat, pre_nat, pre_tab, dens_tab, got_rows, base_ref, slope_ref,
    src, got, summed, col, owned, pull, exc_ref, frac_ref, obs_ref, inv_ref, in_sems, out_sems, up_send, up_recv, down_send, down_recv, *sems,
):
    shell = lax.axis_index("shell")
    me = shell * n_sky + lax.axis_index("sky")
    n_all = n * n_sky
    pairs = (
        (exc_hbm, exc_ref), (frac_hbm, frac_ref), (obs_hbm, obs_ref), (inv_hbm, inv_ref),
    )
    brought = [pltpu.make_async_copy(a, b, in_sems.at[i]) for i, (a, b) in enumerate(pairs)]
    for copy in brought:
        copy.start()
    rows, cols = exc_ref.shape
    tiles, _, width = last4.shape
    blocks = width // LANES
    part = src.shape[1]
    where = lambda p: {"shell": p // n_sky, "sky": lax.rem(p, n_sky)}
    barrier = pltpu.get_barrier_semaphore()
    others(n_all, me, lambda p: pl.semaphore_signal(
        barrier, inc=1, device_id=where(p), device_id_type=pl.DeviceIdType.MESH))
    matrix = stencil_matrix(rows, shell == 0, shell == n - 1)
    brought[0].wait()
    for t in range(tiles):
        at = slice(t * width, (t + 1) * width)
        last4[t] = exc_ref[rows - PASSES :, at]
        first4[t] = exc_ref[:PASSES, at]

    @pl.when(shell == 0)
    def _():
        before[...] = jnp.zeros(before.shape, jnp.float32)

    @pl.when(shell == n - 1)
    def _():
        after[...] = jnp.zeros(after.shape, jnp.float32)

    pl.semaphore_wait(barrier, n_all - 1)

    def upward(t):
        return pltpu.make_async_remote_copy(
            src_ref=last4.at[t], dst_ref=before.at[t], send_sem=up_send.at[t], recv_sem=up_recv.at[t],
            device_id={"shell": lax.rem(shell + 1, n)}, device_id_type=pl.DeviceIdType.MESH,
        )

    def downward(t):
        return pltpu.make_async_remote_copy(
            src_ref=first4.at[t], dst_ref=after.at[t], send_sem=down_send.at[t], recv_sem=down_recv.at[t],
            device_id={"shell": lax.rem(shell + n - 1, n)}, device_id_type=pl.DeviceIdType.MESH,
        )

    has_up, has_down = shell < n - 1, shell > 0

    def send(t, carry):
        pl.when(has_up)(lambda: upward(t).start())
        pl.when(has_down)(lambda: downward(t).start())
        return carry

    lax.fori_loop(0, tiles, send, 0)

    def outward(t):
        at = pl.ds(pl.multiple_of(t * width, width), width)
        return (
            pltpu.make_async_copy(dens_nat.at[t], dens_out.at[:, at], out_sems.at[0, t]),
            pltpu.make_async_copy(pre_nat.at[t], pre_out.at[:, at], out_sems.at[1, t]),
        )

    for copy in brought[1:]:
        copy.wait()
    across = lax.broadcasted_iota(jnp.int32, (rows, 2 * rows), 1)
    across = jnp.where(across >= rows, across - rows, across)
    tri = (across <= lax.broadcasted_iota(jnp.int32, (rows, 2 * rows), 0)).astype(jnp.bfloat16)

    def tile(t, carry):
        pl.when(has_down)(lambda: upward(t).wait_recv())
        pl.when(has_up)(lambda: downward(t).wait_recv())
        e1, e2 = split2(exc_ref[:, pl.ds(pl.multiple_of(t * width, width), width)])
        h1, h2 = split2(jnp.concatenate([before[t], after[t]], 0))
        stacked = jnp.concatenate([e1, e2, h1, h2], 0).astype(jnp.bfloat16)
        both = jnp.dot(matrix, stacked, preferred_element_type=jnp.float32)
        dens = jnp.exp(both[:rows] + both[rows:])
        d1, d2 = split2(dens)
        pre = thickness * jnp.dot(
            tri,
            jnp.concatenate([d1, d2], 0).astype(jnp.bfloat16),
            preferred_element_type=jnp.float32,
        )
        dens_nat[t] = dens
        pre_nat[t] = pre
        for b in range(blocks):
            g = t * blocks + b
            at = pl.ds(pl.multiple_of(g * rows, rows), rows)
            pre_tab[at, :] = pre[:, b * LANES : (b + 1) * LANES]
            dens_tab[at, :] = dens[:, b * LANES : (b + 1) * LANES]
            src[g // part, pl.ds(lax.rem(g, part), 1), :] = pre[rows - 1 :, b * LANES : (b + 1) * LANES]
        for copy in outward(t):
            copy.start()
        return carry

    lax.fori_loop(0, tiles, tile, 0)
    lane = lax.broadcasted_iota(jnp.int32, (LANES, LANES), 1)
    sub = lax.broadcasted_iota(jnp.int32, (LANES, LANES), 0)

    def pick(quad, carry):
        for k in range(4):
            o = quad * 4 + k
            for c in range(LANES):
                at = row_ref[o, c]
                got_rows[k, c : c + 1, :] = pre_tab[pl.ds(at, 1), :]
                got_rows[k, LANES + c : LANES + c + 1, :] = dens_tab[pl.ds(at, 1), :]
        for k in range(4):
            o = quad * 4 + k
            hot = (sub == lo_ref[pl.ds(o, 1), :]).astype(jnp.bfloat16)
            g1, g2 = split2(got_rows[k])
            picked = jnp.dot(
                jnp.concatenate([g1, g2], 0).astype(jnp.bfloat16),
                hot,
                preferred_element_type=jnp.float32,
            )
            p = picked[:LANES] + picked[2 * LANES : 3 * LANES]
            d = picked[LANES : 2 * LANES] + picked[3 * LANES :]
            base_ref[pl.ds(o, 1), :] = jnp.sum(jnp.where(sub == lane, p, 0.0), 0, keepdims=True)
            slope_ref[pl.ds(o, 1), :] = jnp.sum(jnp.where(sub == lane, d, 0.0), 0, keepdims=True)
        return carry

    quads = n_all // 4
    cut = [0, quads // 2, quads]
    shell_exchange(
        n, shell, False, src, got, summed, off_out, sems[:4],
        lambda half: lax.fori_loop(cut[half], cut[half + 1], pick, 0),
    )

    groups = n * src.shape[1]
    o1, o2 = split2(off_out[...].reshape(groups, LANES))
    table = jnp.concatenate([o1.T, o2.T], 0).astype(jnp.bfloat16)
    tall = lax.broadcasted_iota(jnp.int32, (groups, LANES), 0)

    def move(frm, to, send, recv, peer, slot):
        return pltpu.make_async_remote_copy(
            src_ref=frm.at[peer], dst_ref=to.at[slot], send_sem=send.at[peer], recv_sem=recv.at[slot],
            device_id=where(peer), device_id_type=pl.DeviceIdType.MESH,
        )

    send3, recv3, send4, recv4 = sems[4:]

    def push(p):
        pl.when(p != me)(lambda: move(col, owned, send3, recv3, p, me).start())

    def chunk(quad, carry):
        for k in range(4):
            o = quad * 4 + k
            at = pl.ds(o, 1)
            hot = (tall == hi_ref[at, :]).astype(jnp.bfloat16)
            off = jnp.dot(table, hot, preferred_element_type=jnp.float32)
            off = off[:LANES] + off[LANES:]
            off = jnp.sum(jnp.where(sub == lo_ref[at, :], off, 0.0), 0, keepdims=True)
            value = base_ref[at, :] + off - (1.0 - frac_ref[at, :]) * thickness * slope_ref[at, :]
            col[o] = jnp.where(hi_ref[at, :] < groups, value, -1.0)
        for k in range(4):
            push(quad * 4 + k)
        return carry

    lax.fori_loop(0, n_all // 4, chunk, 0)

    owned[pl.ds(me, 1)] = col[pl.ds(me, 1)]
    others(n_all, me, lambda p: move(col, owned, send3, recv3, p, p).wait_recv())
    column = owned[...]
    transmit = jnp.exp(-column)
    inverse = inv_ref[...]
    residual = jnp.where(column > -0.5, (obs_ref[...] - (1.0 - transmit)) * inverse, 0.0)
    res_ref[...] = residual
    pull[...] = jnp.where(column > -0.5, -residual * inverse * transmit, 0.0)
    others(n_all, me, lambda p: move(pull, back_ref, send4, recv4, p, me).start())
    back_ref[pl.ds(me, 1)] = pull[pl.ds(me, 1)]
    others(n_all, me, lambda p: move(pull, back_ref, send4, recv4, p, p).wait_recv())
    others(n_all, me, lambda p: move(col, owned, send3, recv3, p, me).wait_send())
    others(n_all, me, lambda p: move(pull, back_ref, send4, recv4, p, me).wait_send())

    def drain(t, carry):
        for copy in outward(t):
            copy.wait()
        pl.when(has_up)(lambda: upward(t).wait_send())
        pl.when(has_down)(lambda: downward(t).wait_send())
        return carry

    lax.fori_loop(0, tiles, drain, 0)


GROUP = 32
CHUNKS = 4


def scatter_kernel(
    n_own, row_ref, rows_ref, lo_ref, frac_ref, pull_ref, mat_ref, pre_ref, off_ref,
    s_ref, tail_ref, ext_ref, imp_tab, near_tab, upd,
):
    step = pl.program_id(0)
    rows, width = s_ref.shape
    blocks = width // LANES
    first_phase = n_own // CHUNKS

    @pl.when(step == 0)
    def _():
        total = imp_tab.shape[0]

        def clear(i, carry):
            at = pl.ds(pl.multiple_of(i * 256, 256), 256)
            imp_tab[at, :] = jnp.zeros((256, LANES), jnp.float32)
            near_tab[at, :] = jnp.zeros((256, LANES), jnp.float32)
            return carry

        lax.fori_loop(0, total // 256, clear, 0)

    @pl.when(step < first_phase)
    def _():
        ext_ref[...] = pre_ref[...] + off_ref[...]
        sub = lax.broadcasted_iota(jnp.int32, (LANES, LANES), 0)
        lane = lax.broadcasted_iota(jnp.int32, (LANES, LANES), 1)
        grouped = sub // GROUP == lane // GROUP

        for k in range(CHUNKS):
            o = step * CHUNKS + k
            at = pl.ds(o, 1)
            same = jnp.broadcast_to(rows_ref[at, :], (LANES, LANES))
            same = jnp.logical_and(same == same.T, grouped)
            pull = pull_ref[o]
            a1, a2 = split2(jnp.where(same, pull, 0.0))
            b1, b2 = split2(jnp.where(same, pull * (1.0 - frac_ref[at, :]), 0.0))
            hot = (sub == lo_ref[at, :]).astype(jnp.bfloat16)
            out = lax.dot_general(
                jnp.concatenate([a1, a2, b1, b2], 0).astype(jnp.bfloat16),
                hot,
                (((1,), (1,)), ((), ())),
                preferred_element_type=jnp.float32,
            )
            upd[k, :LANES] = out[:LANES] + out[LANES : 2 * LANES]
            upd[k, LANES:] = out[2 * LANES : 3 * LANES] + out[3 * LANES :]
        for k in range(CHUNKS):
            o = step * CHUNKS + k
            for g in range(LANES // GROUP):
                cs = range(g * GROUP, (g + 1) * GROUP)
                where = [row_ref[o, c] for c in cs]
                imps = [imp_tab[pl.ds(w, 1), :] + upd[k, c : c + 1, :] for w, c in zip(where, cs)]
                nears = [near_tab[pl.ds(w, 1), :] + upd[k, LANES + c : LANES + c + 1, :] for w, c in zip(where, cs)]
                for w, a, b in zip(where, imps, nears):
                    imp_tab[pl.ds(w, 1), :] = a
                    near_tab[pl.ds(w, 1), :] = b

    def natural(tab):
        parts = []
        for b in range(blocks):
            at = pl.ds(pl.multiple_of(((step - first_phase) * blocks + b) * rows, rows), rows)
            parts.append(tab[at, :])
        return jnp.concatenate(parts, 1)

    @pl.when(step >= first_phase)
    def _():
        i1, i2 = split2(natural(imp_tab))
        n1, n2 = split2(natural(near_tab))
        out = jnp.dot(
            mat_ref[...],
            jnp.concatenate([i1, i2, n1, n2], 0).astype(jnp.bfloat16),
            preferred_element_type=jnp.float32,
        )
        s_ref[...] = out[:rows]
        tail_ref[...] = out[rows : rows + 1]


def body(excitation, star_shell, star_pixel, star_fraction, star_count, observed, inverse_error):
    rows, cols = excitation.shape
    size = lax.axis_size("shell")
    thickness = depth_span / (rows * size)
    n_own = star_shell.shape[1]
    groups = cols // LANES
    tile = min(TILE, cols)
    f32, bf16 = jnp.float32, jnp.bfloat16

    pixel = star_pixel[0]
    hi, lo = pixel // LANES, pixel % LANES
    row = hi * rows + star_shell[0]
    live = jnp.arange(LANES, dtype=jnp.int32)[None, :] < star_count[0][:, None]
    hi = jnp.where(live, hi, groups)

    smem = pl.BlockSpec(memory_space=pltpu.SMEM)
    vmem = pl.BlockSpec(memory_space=pltpu.VMEM)
    full = lambda shape: pl.BlockSpec(shape, lambda i: (0, 0))
    stars = jax.ShapeDtypeStruct((n_own, LANES), f32)
    grid_shape = jax.ShapeDtypeStruct((rows, cols), f32)
    line = jax.ShapeDtypeStruct((1, cols), f32)
    limit = pltpu.CompilerParams(vmem_limit_bytes=48 * 2**20)

    n_sky = lax.axis_size("sky")
    n_all = size * n_sky
    spread = (size, groups // size, LANES)
    blocks = jax.ShapeDtypeStruct(spread, f32)
    slots = jax.ShapeDtypeStruct((n_all, 1, LANES), f32)
    hold = lambda like: pltpu.VMEM(like.shape, f32)
    dma = lambda k: pltpu.SemaphoreType.DMA((k,))

    def remote(number):
        return pltpu.CompilerParams(
            collective_id=number, has_side_effects=True, vmem_limit_bytes=48 * 2**20
        )

    tiles = cols // tile
    hbm = pl.BlockSpec(memory_space=pl.ANY)
    edge = pltpu.VMEM((tiles, PASSES, tile), f32)
    nat = pltpu.VMEM((tiles, rows, tile), f32)
    tab = pltpu.VMEM((groups * rows, LANES), f32)
    density, prefix, offset, residual, returned = pl.pallas_call(
        lambda *refs: field_kernel(size, n_sky, thickness, *refs),
        in_specs=[smem, vmem, vmem] + [hbm] * 4,
        out_specs=[hbm] * 2 + [vmem] * 3,
        out_shape=[grid_shape, grid_shape, blocks, slots, slots],
        scratch_shapes=[edge] * 4 + [nat] * 2 + [tab] * 2
        + [pltpu.VMEM((4, 2 * LANES, LANES), f32), hold(stars), hold(stars)]
        + [hold(blocks)] * 3 + [hold(slots)] * 3
        + [pltpu.VMEM((rows, cols), f32), hold(stars), hold(slots), hold(slots)]
        + [dma(4), pltpu.SemaphoreType.DMA((2, tiles))] + [dma(tiles)] * 4 + [dma(size)] * 4 + [dma(n_all)] * 4,
        compiler_params=remote(0),
        name="field",
    )(row, hi, lo, excitation, star_fraction[0], observed, inverse_error)

    upper = np.triu(np.ones((rows, rows), np.float32))
    eye = np.eye(rows, dtype=np.float32)
    top_row = np.zeros((16, 4 * rows), np.float32)
    top_row[0, : 2 * rows] = 1.0
    smat = jnp.asarray(
        np.concatenate([np.concatenate([upper, upper, -eye, -eye], 1), top_row], 0).astype(bf16)
    )
    early = n_own // CHUNKS
    ext_tile = cols // early
    out_tile = min(2 * TILE, cols)
    first = lambda r: pl.BlockSpec((r, ext_tile), lambda i: (0, jnp.minimum(i, early - 1)))
    second = lambda r: pl.BlockSpec((r, out_tile), lambda i: (0, jnp.maximum(i - early, 0)))
    local_sens, tails, extinction = pl.pallas_call(
        lambda *refs: scatter_kernel(n_own, *refs),
        grid=(early + cols // out_tile,),
        in_specs=[smem] + [full((n_own, LANES))] * 3
        + [pl.BlockSpec((n_own, 1, LANES), lambda i: (0, 0, 0)), full(smat.shape), first(rows), first(1)],
        out_specs=[second(rows), second(1), first(rows)],
        out_shape=[grid_shape, line, grid_shape],
        scratch_shapes=[
            pltpu.VMEM((groups * rows, LANES), f32),
            pltpu.VMEM((groups * rows, LANES), f32),
            pltpu.VMEM((CHUNKS, 2 * LANES, LANES), f32),
        ],
        compiler_params=limit,
        name="scatter",
    )(row, row.astype(f32), lo, star_fraction[0], returned, smat, prefix, offset.reshape(1, -1))

    tail_offset = pl.pallas_call(
        lambda *refs: tail_kernel(size, *refs),
        in_specs=[vmem],
        out_specs=vmem,
        out_shape=blocks,
        scratch_shapes=[hold(blocks), hold(blocks)] + [dma(size)] * 4,
        compiler_params=remote(1),
        name="tails",
    )(tails.reshape(spread))
    sensitivity = density * (local_sens + tail_offset.reshape(1, -1))
    return extinction, sensitivity, residual


def solution(mesh):
    stars = P(("shell", "sky"), None, None)
    owners = P(None, ("shell", "sky"), None)
    return jax.shard_map(
        body,
        mesh=mesh,
        in_specs=(P("shell", "sky"), stars, stars, stars, P(("shell", "sky"), None), owners, owners),
        out_specs=(P("shell", "sky"), P("shell", "sky"), owners),
        check_vma=False,
    )
```
